32 devices in a mesh: gx: 2 (over x), gy: 4 (over y, core), gz: 4 (over z).
Axes of the slice: x: 2, y: 2, z: 4, core: 2. Of those that a mesh axis runs over, the one named last changes fastest.
Arguments:
- right_side: float32 [32, 256, 512], P('gx', 'gz', 'gy'), may hold values from -8 to 8, as said below
- absorption: float32 [32, 256, 512], P('gx', 'gz', 'gy'), may hold values from 1e-05 to 1, as said below
Outputs:
- fine_iterate: float32 [32, 256, 512], P('gx', 'gz', 'gy')
- middle_iterate: float32 [16, 128, 256], P('gx', 'gz', 'gy')
- corrected_iterate: float32 [8, 64, 128], P('gx', 'gz', 'gy')
The draws below stay inside these ranges and needn't reach their ends.
Inputs may be any that keep to these rules, and one draw needn't show every extreme that they name: `right_side`: independent cell values, possibly with a smooth part added. `absorption`: positive at every cell.
All inputs are finite; a program needn't handle non-finite values.
Results may differ from the reference program's by a relative error of at most 0.0001.
Values sent between devices are 32-bit elements; how exact they have to be, the bound alone decides.
A program may use at most 128 MiB of HBM per device.

```python
import math
import jax
import jax.numpy as jnp
from jax import lax

CX = 16
CY = 128
CZ = 64
DEGREE = 4
LEVELS = 3
BOTTOM_ITERS = 20
NX = 32
NY = 512
NZ = 256


def draw_right_side(key, part):
    noise = jnp.clip(jax.random.normal(key, (NX, NZ, NY), jnp.float32), -6.0, 6.0)
    return noise


def sponge_ramp(count, width):
    positions = jnp.arange(count, dtype=jnp.float32)
    distance = jnp.minimum(positions, count - 1.0 - positions) + 0.5
    return jnp.square(jnp.clip((width - distance) / width, 0.0, 1.0))


def draw_absorption(key, part):
    factor = jnp.exp(jax.random.uniform(key, (NX, NZ, NY), jnp.float32, math.log(0.5), math.log(2.0)))
    along_first = sponge_ramp(NX, CX * 1.0)
    along_second = sponge_ramp(NZ, CZ * 1.0)
    along_third = sponge_ramp(NY, CY * 1.0)
    profile = jnp.maximum(jnp.maximum(along_first[:, None, None], along_second[None, :, None]), along_third[None, None, :])
    return factor * (2e-05 + 0.49998 * profile)


def setup_inputs(seed: int = 0) -> dict:
    splits = jax.random.split(jax.random.key(seed), 3)
    return {
        "right_side": draw_right_side(jax.random.fold_in(splits[2], 71), 0),
        "absorption": draw_absorption(jax.random.fold_in(splits[2], 71), 0),
    }


smooth_low = 1.5
smooth_top = 12.0
absorb_top = 1.0
bottom_low = 0.008


def cheb_tables(count, lower, upper):
    theta = (upper + lower) / 2.0
    delta = (upper - lower) / 2.0
    sigma = theta / delta
    rho_value = 1.0 / sigma
    firsts = []
    seconds = []
    for turn_index in range(count - 1):
        rho_next = 1.0 / (2.0 * sigma - rho_value)
        firsts.append(rho_next * rho_value)
        seconds.append(2.0 * rho_next / delta)
        rho_value = rho_next
    return 1.0 / theta, firsts, seconds


def chebyshev(source, coefficient, count, lower, upper, operate):
    start_scale, firsts, seconds = cheb_tables(count, lower, upper)
    first_table = jnp.asarray(firsts, jnp.float32)
    second_table = jnp.asarray(seconds, jnp.float32)
    direction = source * start_scale

    def turn(turn_index, carry):
        iterate, direction, residual = carry
        residual = residual - operate(direction, coefficient)
        direction = first_table[turn_index] * direction + second_table[turn_index] * residual
        return (iterate + direction, direction, residual)

    iterate, direction, residual = lax.fori_loop(0, count - 1, turn, (direction, direction, source))
    return iterate


def neighbours(padded):
    return (padded[2:, 1:-1, 1:-1] + padded[:-2, 1:-1, 1:-1] + padded[1:-1, 2:, 1:-1]
            + padded[1:-1, :-2, 1:-1] + padded[1:-1, 1:-1, 2:] + padded[1:-1, 1:-1, :-2])


def global_operator(field, coefficient):
    return (6.0 + coefficient) * field - neighbours(jnp.pad(field, 1))


def restrict_four(field):
    first, second, third = field.shape
    blocks = field.reshape(first // 2, 2, second // 2, 2, third // 2, 2)
    return blocks.sum(axis=(1, 3, 5)) * 0.5


def prolong_axis(extended, axis):
    count = extended.shape[axis] - 2
    center = lax.slice_in_dim(extended, 1, count + 1, axis=axis)
    lower = lax.slice_in_dim(extended, 0, count, axis=axis)
    upper = lax.slice_in_dim(extended, 2, count + 2, axis=axis)
    even = 0.75 * center + 0.25 * lower
    odd = 0.75 * center + 0.25 * upper
    stacked = jnp.stack((even, odd), axis=axis + 1)
    shape = list(extended.shape)
    shape[axis] = 2 * count
    return stacked.reshape(shape)


def prolong(extended):
    for axis in range(3):
        extended = prolong_axis(extended, axis)
    return extended


def reference(right_side, absorption):
    source = right_side
    coefficient = absorption
    iterates = []
    for section in range(LEVELS):
        upper_bound = smooth_top + (4.0 ** section) * absorb_top
        iterate = chebyshev(source, coefficient, DEGREE + 1, smooth_low, upper_bound, global_operator)
        residual = source - global_operator(iterate, coefficient)
        iterates.append(iterate)
        source = restrict_four(residual)
        coefficient = restrict_four(coefficient)
    bottom_top = smooth_top + (4.0 ** LEVELS) * absorb_top
    correction = chebyshev(source, coefficient, BOTTOM_ITERS, bottom_low, bottom_top, global_operator)
    corrected = iterates[2] + prolong(jnp.pad(correction, 1))
    return iterates[0], iterates[1], corrected
```

```python
import functools

import jax
import jax.numpy as jnp
from jax import lax
from jax.experimental import pallas as pl
from jax.experimental.pallas import tpu as pltpu
from jax.sharding import PartitionSpec as P

DEGREE = 4
LEVELS = 3
BOTTOM_ITERS = 20
LANES = 128

smooth_low = 1.5
smooth_top = 12.0
absorb_top = 1.0
bottom_low = 0.008

MESH = pl.DeviceIdType.MESH
AXES = ("gx", "gz", "gy")


def cheb_tables(count, lower, upper):
    theta = (upper + lower) / 2.0
    delta = (upper - lower) / 2.0
    sigma = theta / delta
    rho_value = 1.0 / sigma
    firsts = []
    seconds = []
    for turn_index in range(count - 1):
        rho_next = 1.0 / (2.0 * sigma - rho_value)
        firsts.append(rho_next * rho_value)
        seconds.append(2.0 * rho_next / delta)
        rho_value = rho_next
    return (1.0 / theta, firsts, seconds)


def exact_dot(left, right):
    return jnp.dot(
        left, right, precision=lax.Precision.HIGHEST, preferred_element_type=jnp.float32
    )


def lanes_of(shape):
    return lax.broadcasted_iota(jnp.int32, shape, len(shape) - 1)


def rows_of(shape):
    return lax.broadcasted_iota(jnp.int32, shape, len(shape) - 2)


def halving():
    j = rows_of((LANES, LANES))
    i = lanes_of((LANES, LANES))
    return jnp.where(j // 2 == i, jnp.float32(0.5), jnp.float32(0.0))


def trilinear(coarse, fine):
    centre = fine // 2
    other = centre + 2 * (fine % 2) - 1
    return jnp.where(coarse == centre, jnp.float32(0.75), jnp.float32(0.0)) + jnp.where(
        coarse == other, jnp.float32(0.25), jnp.float32(0.0)
    )


def kernel(sizes, blocks, tab, rs, ab, out0, out1, out2, *scratch):
    nx, nz, ny = sizes
    me = {a: lax.axis_index(a) for a in AXES}
    count = dict(zip(AXES, sizes))
    has_lo = {a: me[a] > 0 for a in AXES}
    has_hi = {a: me[a] < count[a] - 1 for a in AXES}

    per_level = 9
    level_refs = [scratch[per_level * k : per_level * (k + 1)] for k in range(LEVELS)]
    rest = scratch[per_level * LEVELS :]
    pairs, gath, src3, coef3, dir3, res3, it3, send_sem, recv_sem, gsend, grecv = rest

    barrier = pltpu.get_barrier_semaphore()
    greeted = 0
    for a in AXES:
        for k in range(1, count[a]):
            pl.semaphore_signal(
                barrier,
                inc=1,
                device_id={a: lax.rem(me[a] + k, count[a])},
                device_id_type=MESH,
            )
            greeted += 1
    pl.semaphore_wait(barrier, greeted)

    half = halving()

    def restrict(read, shape):
        first, second, _ = shape
        for x in range(first // 2):
            pairs[pl.ds(x * second, second), :] = read(2 * x) + read(2 * x + 1)
        total = first // 2 * second // 2
        summed = (
            pairs[pl.ds(0, total, stride=2), :] + pairs[pl.ds(1, total, stride=2), :]
        )
        return exact_dot(summed, half)

    def copies(level, r):
        first, second, _ = blocks[level]
        dirs, faces_z, faces_y, halo_x, halo_z, halo_y = level_refs[level][:6]
        slot = level * (DEGREE + 1) + r
        ends = {
            "gx": (dirs.at[r, 1], dirs.at[r, first], halo_x),
            "gz": (faces_z.at[r, 0], faces_z.at[r, 1], halo_z),
            "gy": (faces_y.at[r], faces_y.at[r], halo_y),
        }
        made = []
        for n, a in enumerate(AXES):
            low_face, high_face, halo = ends[a]
            made.append(
                (
                    has_lo[a],
                    has_hi[a],
                    pltpu.make_async_remote_copy(
                        src_ref=low_face,
                        dst_ref=halo.at[r, 1],
                        send_sem=send_sem.at[slot, 2 * n],
                        recv_sem=recv_sem.at[slot, 2 * n],
                        device_id={a: jnp.maximum(me[a] - 1, 0)},
                        device_id_type=MESH,
                    ),
                )
            )
            made.append(
                (
                    has_hi[a],
                    has_lo[a],
                    pltpu.make_async_remote_copy(
                        src_ref=high_face,
                        dst_ref=halo.at[r, 0],
                        send_sem=send_sem.at[slot, 2 * n + 1],
                        recv_sem=recv_sem.at[slot, 2 * n + 1],
                        device_id={a: jnp.minimum(me[a] + 1, count[a] - 1)},
                        device_id_type=MESH,
                    ),
                )
            )
        return made

    def start(level, r):
        for sends, _, copy in copies(level, r):
            pl.when(sends)(copy.start)

    def arrive(level, r):
        for _, gets, copy in copies(level, r):
            pl.when(gets)(copy.wait_recv)

    def sent(level, r):
        for sends, _, copy in copies(level, r):
            pl.when(sends)(copy.wait_send)

    def put_faces(level, r, x, field, packed):
        second, width = blocks[level][1:]
        dirs, faces_z = level_refs[level][:2]
        dirs[r, x + 1] = field
        faces_z[r, 0, pl.ds(x, 1), :] = field[:1]
        faces_z[r, 1, pl.ds(x, 1), :] = field[second - 1 :]
        lane = lanes_of((second, LANES))
        low = pltpu.roll(field, 2 * x + 1, 1)
        if width == LANES:
            return jnp.where(lane // 2 == x, low, packed)
        high = pltpu.roll(field, 2 * x + LANES + 1 - width, 1)
        return jnp.where(lane == 2 * x + 1, low, jnp.where(lane == 2 * x, high, packed))

    def inside(level, r, base, coef):
        first, second, width = blocks[level]
        dirs = level_refs[level][0]
        resid = level_refs[level][6]
        row = rows_of((second, LANES))
        lane = lanes_of((second, LANES))

        @pl.loop(0, first)
        def _(x):
            d = dirs[r, x + 1]
            near = dirs[r, x] + dirs[r, x + 2]
            near += jnp.where(row == 0, 0.0, pltpu.roll(d, 1, 0))
            near += jnp.where(row == second - 1, 0.0, pltpu.roll(d, second - 1, 0))
            near += pltpu.roll(d, 1, 1) + pltpu.roll(d, LANES - 1, 1)
            if width < LANES:
                near = jnp.where(lane < width, near, 0.0)
            resid[x] = base[x] - ((6.0 + coef[x]) * d - near)

    def outside(level, r):
        first, second, width = blocks[level]
        faces_y, halo_x, halo_z, halo_y = level_refs[level][2:6]
        resid = level_refs[level][6]
        row = rows_of((second, LANES))
        lane = lanes_of((second, LANES))
        resid[0] += jnp.where(has_lo["gx"], halo_x[r, 0], 0.0)
        resid[first - 1] += jnp.where(has_hi["gx"], halo_x[r, 1], 0.0)
        low = jnp.where(has_lo["gy"], halo_y[r, 0], 0.0)
        high = jnp.where(has_hi["gy"], halo_y[r, 1], 0.0)
        if width == LANES:
            low -= faces_y[r]
            high -= faces_y[r]
        ends = jnp.where(lane % 2 == 1, pltpu.roll(low, 1, 1), pltpu.roll(high, LANES - 1, 1))

        def add(x):
            res = resid[x]
            z_low = jnp.where(has_lo["gz"], halo_z[r, 0, pl.ds(x, 1), :], 0.0)
            z_high = jnp.where(has_hi["gz"], halo_z[r, 1, pl.ds(x, 1), :], 0.0)
            res += jnp.where(row == 0, z_low, 0.0) + jnp.where(row == second - 1, z_high, 0.0)
            to_low = pltpu.roll(ends, LANES - 1 - 2 * x, 1)
            if width == LANES:
                res += jnp.where((lane == 0) | (lane == LANES - 1), to_low, 0.0)
            else:
                to_high = pltpu.roll(ends, width - 1 - 2 * x, 1)
                res += jnp.where(lane == 0, to_low, jnp.where(lane == width - 1, to_high, 0.0))
            return res

        return add

    def pack_zero(level):
        return jnp.zeros((blocks[level][1], LANES), jnp.float32)

    def smooth(level, source, coef, between):
        first, second, width = blocks[level]
        dirs, _, faces_y = level_refs[level][:3]
        resid, iterate = level_refs[level][6:8]
        upper = smooth_top + 4.0**level * absorb_top
        scale, firsts, seconds = cheb_tables(DEGREE + 1, smooth_low, upper)
        empty = jnp.zeros((second, LANES), jnp.float32)
        for r in range(DEGREE + 1):
            dirs[r, 0] = empty
            dirs[r, first + 1] = empty

        def opening(x, packed):
            d = source[x] * scale
            iterate[x] = d
            return put_faces(level, 0, x, d, packed)

        faces_y[0] = lax.fori_loop(0, first, opening, empty)
        for r in range(DEGREE + 1):
            start(level, r)
            inside(level, r, source if r in (0, DEGREE) else resid, coef)
            if r == 0:
                between()
            arrive(level, r)
            add = outside(level, r)
            if r == DEGREE:

                @pl.loop(0, first)
                def _(x):
                    resid[x] = add(x)

            else:

                def turn(x, packed, r=r, add=add):
                    res = add(x)
                    resid[x] = res
                    d = firsts[r] * dirs[r, x + 1] + seconds[r] * res
                    total = iterate[x] + d
                    iterate[x] = total
                    return put_faces(level, r + 1, x, total if r == DEGREE - 1 else d, packed)

                faces_y[r + 1] = lax.fori_loop(0, first, turn, empty)

    bottom = tuple(s // 2 for s in blocks[-1])
    coefs = [ab] + [level_refs[k][8] for k in range(1, LEVELS)]
    sources = [rs] + [level_refs[k][8] for k in range(1, LEVELS)]
    coefs = [ab, level_refs[1][8].at[0], level_refs[2][8].at[0]]
    sources = [rs, level_refs[1][8].at[1], level_refs[2][8].at[1]]
    message = gath.at[me["gx"], me["gy"], me["gz"]]

    def spread(rows, shape, ref):
        for x in range(shape[0]):
            ref[x] = rows[x * shape[1] : (x + 1) * shape[1]]

    def into_message(rows, first_part):
        packed = jnp.zeros((bottom[1], LANES), jnp.float32)
        for x in range(bottom[0]):
            part = rows[x * bottom[1] : (x + 1) * bottom[1]]
            shift = (first_part + x) * bottom[2]
            packed += pltpu.roll(part, shift, 1) if shift else part
        return packed

    def coarsen():
        for level in range(1, LEVELS):
            rows = restrict(lambda x: coefs[level - 1][x], blocks[level - 1])
            spread(rows, blocks[level], coefs[level])
        rows = restrict(lambda x: coefs[LEVELS - 1][x], blocks[LEVELS - 1])
        message[...] = into_message(rows, bottom[0])

    for level in range(LEVELS):
        smooth(level, sources[level], coefs[level], coarsen if level == 0 else lambda: None)
        resid = level_refs[level][6]
        rows = restrict(lambda x: resid[x], blocks[level])
        if level + 1 < LEVELS:
            spread(rows, blocks[level + 1], sources[level + 1])
    message[...] += into_message(rows, 0)

    pieces = {
        "gz": message,
        "gx": gath.at[me["gx"], me["gy"]],
        "gy": gath.at[:, me["gy"]],
    }
    base = 0
    for a in ("gz", "gx", "gy"):
        made = []
        for k in range(1, count[a]):
            made.append(
                pltpu.make_async_remote_copy(
                    src_ref=pieces[a],
                    dst_ref=pieces[a],
                    send_sem=gsend.at[base],
                    recv_sem=grecv.at[base],
                    device_id={a: lax.rem(me[a] + k, count[a])},
                    device_id_type=MESH,
                )
            )
            base += 1
        for copy in made:
            copy.start()
        for copy in made:
            copy.wait_recv()
        for copy in made:
            copy.wait_send()

    bx, bz, by = bottom
    whole_x, whole_z, whole_y = bx * nx, bz * nz, by * ny
    lane = lanes_of((bz, LANES))

    def place(n, carry):
        ix = n // nz
        iz = n % nz
        for part, ref in ((0, src3), (bx, coef3)):
            for x in range(bx):
                tile = jnp.zeros((bz, LANES), jnp.float32)
                for iy in range(ny):
                    shift = (iy - part - x) * by % LANES
                    moved = gath[ix, iy, iz]
                    if shift:
                        moved = pltpu.roll(moved, shift, 1)
                    tile = jnp.where(lane // by == iy, moved, tile)
                ref[ix * bx + x, pl.ds(pl.multiple_of(iz * bz, bz), bz), :] = tile
        return carry

    lax.fori_loop(0, nx * nz, place, 0)

    upper = smooth_top + 4.0**LEVELS * absorb_top
    scale = cheb_tables(BOTTOM_ITERS, bottom_low, upper)[0]
    zero = jnp.zeros((whole_z, LANES), jnp.float32)
    row = rows_of((whole_z, LANES))
    lane = lanes_of((whole_z, LANES))
    for ref in (dir3, it3):
        ref[0] = zero
        ref[whole_x + 1] = zero
    for x in range(whole_x):
        source = src3[x]
        res3[x] = source
        dir3[x + 1] = source * scale
        it3[x + 1] = source * scale

    def bottom_turn(n, carry):
        one = tab[0, n]
        two = tab[1, n]
        layers = [dir3[x] for x in range(whole_x + 2)]
        for x in range(whole_x):
            d = layers[x + 1]
            near = layers[x] + layers[x + 2]
            near += jnp.where(row == 0, 0.0, pltpu.roll(d, 1, 0))
            near += jnp.where(row == whole_z - 1, 0.0, pltpu.roll(d, whole_z - 1, 0))
            if whole_y < LANES:
                near += pltpu.roll(d, 1, 1) + pltpu.roll(d, LANES - 1, 1)
                near = jnp.where(lane < whole_y, near, 0.0)
            else:
                near += jnp.where(lane == 0, 0.0, pltpu.roll(d, 1, 1))
                near += jnp.where(lane == LANES - 1, 0.0, pltpu.roll(d, LANES - 1, 1))
            res = res3[x] - ((6.0 + coef3[x]) * d - near)
            res3[x] = res
            d = one * d + two * res
            dir3[x + 1] = d
            it3[x + 1] += d
        return carry

    lax.fori_loop(0, BOTTOM_ITERS - 1, bottom_turn, 0)

    first, second, width = blocks[-1]
    i = lanes_of((LANES, LANES))
    along_y = jnp.where(
        i < width, trilinear(rows_of((LANES, LANES)), me["gy"] * width + i), 0.0
    )
    along_z = trilinear(
        lanes_of((second, whole_z)), me["gz"] * second + rows_of((second, whole_z))
    )
    layers = []
    for x in range(first):
        centre = me["gx"] * (first // 2) + x // 2 + 1
        layers.append(0.75 * it3[centre] + 0.25 * it3[centre + 2 * (x % 2) - 1])
    moved = exact_dot(jnp.concatenate(layers, axis=0), along_y)
    iterate = level_refs[-1][7]
    for x in range(first):
        fine = exact_dot(along_z, moved[x * whole_z : (x + 1) * whole_z])
        out2[x] = (iterate[x] + fine)[:, :width]

    first, second, width = blocks[0]

    @pl.loop(0, first)
    def _(x):
        out0[x] = level_refs[0][7][x]

    first, second, width = blocks[1]
    for x in range(first):
        out1[x] = level_refs[1][7][x][:, :width]

    for level in range(LEVELS):
        for r in range(DEGREE + 1):
            sent(level, r)


def on_device(sizes, right_side, absorption):
    nx, nz, ny = sizes
    blocks = [tuple(s // 2**k for s in right_side.shape) for k in range(LEVELS)]
    rounds = DEGREE + 1
    scratch = []
    for first, second, width in blocks:
        scratch += [
            pltpu.VMEM((rounds, first + 2, second, LANES), jnp.float32),
            pltpu.VMEM((rounds, 2, first, LANES), jnp.float32),
            pltpu.VMEM((rounds, second, LANES), jnp.float32),
            pltpu.VMEM((rounds, 2, second, LANES), jnp.float32),
            pltpu.VMEM((rounds, 2, first, LANES), jnp.float32),
            pltpu.VMEM((rounds, 2, second, LANES), jnp.float32),
            pltpu.VMEM((first, second, LANES), jnp.float32),
            pltpu.VMEM((first, second, LANES), jnp.float32),
            pltpu.VMEM((2, first, second, LANES), jnp.float32),
        ]
    bx, bz, by = (s // 2 for s in blocks[-1])
    whole = (bx * nx, bz * nz, LANES)
    padded = (bx * nx + 2, bz * nz, LANES)
    lines = nx + ny + nz - 3
    scratch += [
        pltpu.VMEM((blocks[0][0] // 2 * blocks[0][1], LANES), jnp.float32),
        pltpu.VMEM((nx, ny, nz, bz, LANES), jnp.float32),
        pltpu.VMEM(whole, jnp.float32),
        pltpu.VMEM(whole, jnp.float32),
        pltpu.VMEM(padded, jnp.float32),
        pltpu.VMEM(whole, jnp.float32),
        pltpu.VMEM(padded, jnp.float32),
        pltpu.SemaphoreType.DMA((LEVELS * rounds, 6)),
        pltpu.SemaphoreType.DMA((LEVELS * rounds, 6)),
        pltpu.SemaphoreType.DMA((lines,)),
        pltpu.SemaphoreType.DMA((lines,)),
    ]
    upper = smooth_top + 4.0**LEVELS * absorb_top
    _, firsts, seconds = cheb_tables(BOTTOM_ITERS, bottom_low, upper)
    table = jnp.asarray([firsts, seconds], jnp.float32)
    vmem = pl.BlockSpec(memory_space=pltpu.VMEM)
    return pl.pallas_call(
        functools.partial(kernel, sizes, blocks),
        out_shape=tuple(jax.ShapeDtypeStruct(b, jnp.float32) for b in blocks),
        in_specs=[pl.BlockSpec(memory_space=pltpu.SMEM), vmem, vmem],
        out_specs=(vmem, vmem, vmem),
        scratch_shapes=scratch,
        compiler_params=pltpu.CompilerParams(
            collective_id=0, has_side_effects=True, vmem_limit_bytes=48 * 1024 * 1024
        ),
    )(table, right_side, absorption)


def solution(mesh):
    sizes = tuple(mesh.shape[a] for a in AXES)
    spec = P("gx", "gz", "gy")
    return jax.shard_map(
        functools.partial(on_device, sizes),
        mesh=mesh,
        in_specs=(spec, spec),
        out_specs=(spec, spec, spec),
        check_vma=False,
    )
```

```python
import functools

import jax
import jax.numpy as jnp
from jax import lax
from jax.experimental import pallas as pl
from jax.experimental.pallas import tpu as pltpu
from jax.sharding import PartitionSpec as P

DEGREE = 4
LEVELS = 3
BOTTOM_ITERS = 20
LANES = 128

smooth_low = 1.5
smooth_top = 12.0
absorb_top = 1.0
bottom_low = 0.008

MESH = pl.DeviceIdType.MESH
AXES = ("gx", "gz", "gy")


def cheb_tables(count, lower, upper):
    theta = (upper + lower) / 2.0
    delta = (upper - lower) / 2.0
    sigma = theta / delta
    rho_value = 1.0 / sigma
    firsts = []
    seconds = []
    for turn_index in range(count - 1):
        rho_next = 1.0 / (2.0 * sigma - rho_value)
        firsts.append(rho_next * rho_value)
        seconds.append(2.0 * rho_next / delta)
        rho_value = rho_next
    return (1.0 / theta, firsts, seconds)


def exact_dot(left, right):
    return jnp.dot(
        left, right, precision=lax.Precision.HIGHEST, preferred_element_type=jnp.float32
    )


def lanes_of(shape):
    return lax.broadcasted_iota(jnp.int32, shape, len(shape) - 1)


def rows_of(shape):
    return lax.broadcasted_iota(jnp.int32, shape, len(shape) - 2)


def halving():
    j = rows_of((LANES, LANES))
    i = lanes_of((LANES, LANES))
    return jnp.where(j // 2 == i, jnp.float32(0.5), jnp.float32(0.0))


def trilinear(coarse, fine):
    centre = fine // 2
    other = centre + 2 * (fine % 2) - 1
    return jnp.where(coarse == centre, jnp.float32(0.75), jnp.float32(0.0)) + jnp.where(
        coarse == other, jnp.float32(0.25), jnp.float32(0.0)
    )


def kernel(sizes, blocks, tab, rs, ab, out0, out1, out2, *scratch):
    nx, nz, ny = sizes
    me = {a: lax.axis_index(a) for a in AXES}
    count = dict(zip(AXES, sizes))
    has_lo = {a: me[a] > 0 for a in AXES}
    has_hi = {a: me[a] < count[a] - 1 for a in AXES}

    per_level = 9
    level_refs = [list(scratch[per_level * k : per_level * (k + 1)]) for k in range(LEVELS)]
    level_refs[0][7] = out0
    rest = scratch[per_level * LEVELS :]
    pairs, gath, src3, coef3, dir3, res3, it3, send_sem, recv_sem, gsend, grecv = rest

    barrier = pltpu.get_barrier_semaphore()
    greeted = 0
    for a in AXES:
        for k in range(1, count[a]):
            pl.semaphore_signal(
                barrier,
                inc=1,
                device_id={a: lax.rem(me[a] + k, count[a])},
                device_id_type=MESH,
            )
            greeted += 1
    pl.semaphore_wait(barrier, greeted)

    half = halving()

    def restrict(read, shape):
        first, second, _ = shape
        for x in range(first // 2):
            pairs[pl.ds(x * second, second), :] = read(2 * x) + read(2 * x + 1)
        total = first // 2 * second // 2
        summed = (
            pairs[pl.ds(0, total, stride=2), :] + pairs[pl.ds(1, total, stride=2), :]
        )
        return exact_dot(summed, half)

    def copies(level, r):
        first, second, _ = blocks[level]
        dirs, faces_z, faces_y, halo_x, halo_z, halo_y = level_refs[level][:6]
        slot = level * (DEGREE + 1) + r
        ends = {
            "gx": (dirs.at[r, 1], dirs.at[r, first], halo_x),
            "gz": (faces_z.at[r, 0], faces_z.at[r, 1], halo_z),
            "gy": (faces_y.at[r], faces_y.at[r], halo_y),
        }
        made = []
        for n, a in enumerate(AXES):
            low_face, high_face, halo = ends[a]
            made.append(
                (
                    has_lo[a],
                    has_hi[a],
                    pltpu.make_async_remote_copy(
                        src_ref=low_face,
                        dst_ref=halo.at[r, 1],
                        send_sem=send_sem.at[slot, 2 * n],
                        recv_sem=recv_sem.at[slot, 2 * n],
                        device_id={a: jnp.maximum(me[a] - 1, 0)},
                        device_id_type=MESH,
                    ),
                )
            )
            made.append(
                (
                    has_hi[a],
                    has_lo[a],
                    pltpu.make_async_remote_copy(
                        src_ref=high_face,
                        dst_ref=halo.at[r, 0],
                        send_sem=send_sem.at[slot, 2 * n + 1],
                        recv_sem=recv_sem.at[slot, 2 * n + 1],
                        device_id={a: jnp.minimum(me[a] + 1, count[a] - 1)},
                        device_id_type=MESH,
                    ),
                )
            )
        return made

    def start(level, r):
        for sends, _, copy in copies(level, r):
            pl.when(sends)(copy.start)

    def arrive(level, r):
        for _, gets, copy in copies(level, r):
            pl.when(gets)(copy.wait_recv)

    def sent(level, r):
        for sends, _, copy in copies(level, r):
            pl.when(sends)(copy.wait_send)

    def put_faces(level, r, x, field, packed):
        second, width = blocks[level][1:]
        dirs, faces_z = level_refs[level][:2]
        dirs[r, x + 1] = field
        faces_z[r, 0, pl.ds(x, 1), :] = field[:1]
        faces_z[r, 1, pl.ds(x, 1), :] = field[second - 1 :]
        lane = lanes_of((second, LANES))
        low = pltpu.roll(field, 2 * x + 1, 1)
        if width == LANES:
            return jnp.where(lane // 2 == x, low, packed)
        high = pltpu.roll(field, 2 * x + LANES + 1 - width, 1)
        return jnp.where(lane == 2 * x + 1, low, jnp.where(lane == 2 * x, high, packed))

    def by_chunks(level, body, carry):
        first, second, _ = blocks[level]
        chunk = min(first, 256 // second)

        def turn(n, carry):
            return body([n * chunk + j for j in range(chunk)], carry)

        if chunk == first:
            return turn(0, carry)
        return lax.fori_loop(0, first // chunk, turn, carry)

    edge_row = rows_of((8, LANES))

    def inside(level, r, base, coef):
        first, second, width = blocks[level]
        dirs = level_refs[level][0]
        resid = level_refs[level][6]
        lane = lanes_of((second, LANES))

        def body(xs, carry):
            layers = [dirs[r, xs[0] + j] for j in range(len(xs) + 2)]
            bases = [base[x] for x in xs]
            parts = [coef[x] for x in xs]
            results = []
            for j in range(len(xs)):
                d = layers[j + 1]
                near = layers[j] + layers[j + 2]
                up = pltpu.roll(d, 1, 0)
                down = pltpu.roll(d, second - 1, 0)
                up = jnp.concatenate((jnp.where(edge_row == 0, 0.0, up[:8]), up[8:]), 0)
                down = jnp.concatenate(
                    (down[: second - 8], jnp.where(edge_row == 7, 0.0, down[second - 8 :])), 0
                )
                near += up + down
                near += pltpu.roll(d, 1, 1) + pltpu.roll(d, LANES - 1, 1)
                if width < LANES:
                    near = jnp.where(lane < width, near, 0.0)
                results.append(bases[j] - ((6.0 + parts[j]) * d - near))
            for j, x in enumerate(xs):
                resid[x] = results[j]
            return carry

        by_chunks(level, body, 0)

    def outside(level, r):
        first, second, width = blocks[level]
        faces_y, halo_x, halo_z, halo_y = level_refs[level][2:6]
        resid = level_refs[level][6]
        lane = lanes_of((second, LANES))
        resid[0] += jnp.where(has_lo["gx"], halo_x[r, 0], 0.0)
        resid[first - 1] += jnp.where(has_hi["gx"], halo_x[r, 1], 0.0)
        low = jnp.where(has_lo["gy"], halo_y[r, 0], 0.0)
        high = jnp.where(has_hi["gy"], halo_y[r, 1], 0.0)
        if width == LANES:
            low -= faces_y[r]
            high -= faces_y[r]
        ends = jnp.where(lane % 2 == 1, pltpu.roll(low, 1, 1), pltpu.roll(high, LANES - 1, 1))

        def add(x):
            res = resid[x]
            z_low = jnp.where(has_lo["gz"], halo_z[r, 0, pl.ds(x, 1), :], 0.0)
            z_high = jnp.where(has_hi["gz"], halo_z[r, 1, pl.ds(x, 1), :], 0.0)
            res = jnp.concatenate(
                (
                    res[:8] + jnp.where(edge_row == 0, z_low, 0.0),
                    res[8 : second - 8],
                    res[second - 8 :] + jnp.where(edge_row == 7, z_high, 0.0),
                )[:: 1 if second > 16 else 2],
                0,
            )
            to_low = pltpu.roll(ends, LANES - 1 - 2 * x, 1)
            if width == LANES:
                res += jnp.where((lane == 0) | (lane == LANES - 1), to_low, 0.0)
            else:
                to_high = pltpu.roll(ends, width - 1 - 2 * x, 1)
                res += jnp.where(lane == 0, to_low, jnp.where(lane == width - 1, to_high, 0.0))
            return res

        return add

    def smooth(level, source, coef, between):
        first, second, width = blocks[level]
        dirs, _, faces_y = level_refs[level][:3]
        resid, iterate = level_refs[level][6:8]
        upper = smooth_top + 4.0**level * absorb_top
        scale, firsts, seconds = cheb_tables(DEGREE + 1, smooth_low, upper)
        empty = jnp.zeros((second, LANES), jnp.float32)
        for r in range(DEGREE + 1):
            dirs[r, 0] = empty
            dirs[r, first + 1] = empty

        def opening(xs, packed):
            fields = [source[x] * scale for x in xs]
            for x, d in zip(xs, fields):
                iterate[x] = d
                packed = put_faces(level, 0, x, d, packed)
            return packed

        faces_y[0] = by_chunks(level, opening, empty)
        for r in range(DEGREE + 1):
            start(level, r)
            inside(level, r, source if r in (0, DEGREE) else resid, coef)
            if r == 0:
                between()
            arrive(level, r)
            add = outside(level, r)

            def last(xs, carry, add=add):
                results = [add(x) for x in xs]
                for x, res in zip(xs, results):
                    resid[x] = res
                return carry

            def turn(xs, packed, r=r, add=add):
                results = [add(x) for x in xs]
                fields = [
                    firsts[r] * dirs[r, x + 1] + seconds[r] * res for x, res in zip(xs, results)
                ]
                totals = [iterate[x] + d for x, d in zip(xs, fields)]
                for x, res, d, total in zip(xs, results, fields, totals):
                    resid[x] = res
                    iterate[x] = total
                    packed = put_faces(
                        level, r + 1, x, total if r == DEGREE - 1 else d, packed
                    )
                return packed

            if r == DEGREE:
                by_chunks(level, last, 0)
            else:
                faces_y[r + 1] = by_chunks(level, turn, empty)

    bottom = tuple(s // 2 for s in blocks[-1])
    coefs = [ab, level_refs[1][8].at[0], level_refs[2][8].at[0]]
    sources = [rs, level_refs[1][8].at[1], level_refs[2][8].at[1]]
    message = gath.at[me["gx"], me["gy"], me["gz"]]

    def spread(rows, shape, ref):
        for x in range(shape[0]):
            ref[x] = rows[x * shape[1] : (x + 1) * shape[1]]

    def into_message(rows, first_part):
        packed = jnp.zeros((bottom[1], LANES), jnp.float32)
        for x in range(bottom[0]):
            part = rows[x * bottom[1] : (x + 1) * bottom[1]]
            shift = (first_part + x) * bottom[2]
            packed += pltpu.roll(part, shift, 1) if shift else part
        return packed

    def coarsen():
        for level in range(1, LEVELS):
            rows = restrict(lambda x: coefs[level - 1][x], blocks[level - 1])
            spread(rows, blocks[level], coefs[level])
        rows = restrict(lambda x: coefs[LEVELS - 1][x], blocks[LEVELS - 1])
        message[...] = into_message(rows, bottom[0])

    for level in range(LEVELS):
        smooth(level, sources[level], coefs[level], coarsen if level == 0 else lambda: None)
        resid = level_refs[level][6]
        rows = restrict(lambda x: resid[x], blocks[level])
        if level + 1 < LEVELS:
            spread(rows, blocks[level + 1], sources[level + 1])
    message[...] += into_message(rows, 0)

    pieces = {
        "gz": message,
        "gx": gath.at[me["gx"], me["gy"]],
        "gy": gath.at[:, me["gy"]],
    }
    base = 0
    for a in ("gz", "gx", "gy"):
        made = []
        for k in range(1, count[a]):
            made.append(
                pltpu.make_async_remote_copy(
                    src_ref=pieces[a],
                    dst_ref=pieces[a],
                    send_sem=gsend.at[base],
                    recv_sem=grecv.at[base],
                    device_id={a: lax.rem(me[a] + k, count[a])},
                    device_id_type=MESH,
                )
            )
            base += 1
        for copy in made:
            copy.start()
        for copy in made:
            copy.wait_recv()
        for copy in made:
            copy.wait_send()

    bx, bz, by = bottom
    whole_x, whole_z, whole_y = bx * nx, bz * nz, by * ny
    lane = lanes_of((bz, LANES))

    def place(n, carry):
        ix = n // nz
        iz = n % nz
        for part, ref in ((0, src3), (bx, coef3)):
            for x in range(bx):
                tile = jnp.zeros((bz, LANES), jnp.float32)
                for iy in range(ny):
                    shift = (iy - part - x) * by % LANES
                    moved = gath[ix, iy, iz]
                    if shift:
                        moved = pltpu.roll(moved, shift, 1)
                    tile = jnp.where(lane // by == iy, moved, tile)
                ref[ix * bx + x, pl.ds(pl.multiple_of(iz * bz, bz), bz), :] = tile
        return carry

    lax.fori_loop(0, nx * nz, place, 0)

    upper = smooth_top + 4.0**LEVELS * absorb_top
    scale = cheb_tables(BOTTOM_ITERS, bottom_low, upper)[0]
    zero = jnp.zeros((whole_z, LANES), jnp.float32)
    row = rows_of((whole_z, LANES))
    lane = lanes_of((whole_z, LANES))
    for ref in (dir3, it3):
        ref[0] = zero
        ref[whole_x + 1] = zero
    for x in range(whole_x):
        source = src3[x]
        res3[x] = source
        dir3[x + 1] = source * scale
        it3[x + 1] = source * scale

    def bottom_turn(n, carry):
        one = tab[0, n]
        two = tab[1, n]
        layers = [dir3[x] for x in range(whole_x + 2)]
        for x in range(whole_x):
            d = layers[x + 1]
            near = layers[x] + layers[x + 2]
            near += jnp.where(row == 0, 0.0, pltpu.roll(d, 1, 0))
            near += jnp.where(row == whole_z - 1, 0.0, pltpu.roll(d, whole_z - 1, 0))
            if whole_y < LANES:
                near += pltpu.roll(d, 1, 1) + pltpu.roll(d, LANES - 1, 1)
                near = jnp.where(lane < whole_y, near, 0.0)
            else:
                near += jnp.where(lane == 0, 0.0, pltpu.roll(d, 1, 1))
                near += jnp.where(lane == LANES - 1, 0.0, pltpu.roll(d, LANES - 1, 1))
            res = res3[x] - ((6.0 + coef3[x]) * d - near)
            res3[x] = res
            d = one * d + two * res
            dir3[x + 1] = d
            it3[x + 1] += d
        return carry

    lax.fori_loop(0, BOTTOM_ITERS - 1, bottom_turn, 0)

    first, second, width = blocks[-1]
    i = lanes_of((LANES, LANES))
    along_y = jnp.where(
        i < width, trilinear(rows_of((LANES, LANES)), me["gy"] * width + i), 0.0
    )
    along_z = trilinear(
        lanes_of((second, whole_z)), me["gz"] * second + rows_of((second, whole_z))
    )
    layers = []
    for x in range(first):
        centre = me["gx"] * (first // 2) + x // 2 + 1
        layers.append(0.75 * it3[centre] + 0.25 * it3[centre + 2 * (x % 2) - 1])
    moved = exact_dot(jnp.concatenate(layers, axis=0), along_y)
    iterate = level_refs[-1][7]
    for x in range(first):
        fine = exact_dot(along_z, moved[x * whole_z : (x + 1) * whole_z])
        out2[x] = (iterate[x] + fine)[:, :width]

    first, second, width = blocks[1]
    for x in range(first):
        out1[x] = level_refs[1][7][x][:, :width]

    for level in range(LEVELS):
        for r in range(DEGREE + 1):
            sent(level, r)


def on_device(sizes, right_side, absorption):
    nx, nz, ny = sizes
    blocks = [tuple(s // 2**k for s in right_side.shape) for k in range(LEVELS)]
    rounds = DEGREE + 1
    scratch = []
    for first, second, width in blocks:
        scratch += [
            pltpu.VMEM((rounds, first + 2, second, LANES), jnp.float32),
            pltpu.VMEM((rounds, 2, first, LANES), jnp.float32),
            pltpu.VMEM((rounds, second, LANES), jnp.float32),
            pltpu.VMEM((rounds, 2, second, LANES), jnp.float32),
            pltpu.VMEM((rounds, 2, first, LANES), jnp.float32),
            pltpu.VMEM((rounds, 2, second, LANES), jnp.float32),
            pltpu.VMEM((first, second, LANES), jnp.float32),
            pltpu.VMEM((first, second, LANES), jnp.float32),
            pltpu.VMEM((2, first, second, LANES), jnp.float32),
        ]
    bx, bz, by = (s // 2 for s in blocks[-1])
    whole = (bx * nx, bz * nz, LANES)
    padded = (bx * nx + 2, bz * nz, LANES)
    lines = nx + ny + nz - 3
    scratch += [
        pltpu.VMEM((blocks[0][0] // 2 * blocks[0][1], LANES), jnp.float32),
        pltpu.VMEM((nx, ny, nz, bz, LANES), jnp.float32),
        pltpu.VMEM(whole, jnp.float32),
        pltpu.VMEM(whole, jnp.float32),
        pltpu.VMEM(padded, jnp.float32),
        pltpu.VMEM(whole, jnp.float32),
        pltpu.VMEM(padded, jnp.float32),
        pltpu.SemaphoreType.DMA((LEVELS * rounds, 6)),
        pltpu.SemaphoreType.DMA((LEVELS * rounds, 6)),
        pltpu.SemaphoreType.DMA((lines,)),
        pltpu.SemaphoreType.DMA((lines,)),
    ]
    upper = smooth_top + 4.0**LEVELS * absorb_top
    _, firsts, seconds = cheb_tables(BOTTOM_ITERS, bottom_low, upper)
    table = jnp.asarray([firsts, seconds], jnp.float32)
    vmem = pl.BlockSpec(memory_space=pltpu.VMEM)
    return pl.pallas_call(
        functools.partial(kernel, sizes, blocks),
        out_shape=tuple(jax.ShapeDtypeStruct(b, jnp.float32) for b in blocks),
        in_specs=[pl.BlockSpec(memory_space=pltpu.SMEM), vmem, vmem],
        out_specs=(vmem, vmem, vmem),
        scratch_shapes=scratch,
        compiler_params=pltpu.CompilerParams(
            collective_id=0, has_side_effects=True, vmem_limit_bytes=48 * 1024 * 1024
        ),
    )(table, right_side, absorption)


def solution(mesh):
    sizes = tuple(mesh.shape[a] for a in AXES)
    spec = P("gx", "gz", "gy")
    return jax.shard_map(
        functools.partial(on_device, sizes),
        mesh=mesh,
        in_specs=(spec, spec),
        out_specs=(spec, spec, spec),
        check_vma=False,
    )
```

```python
import functools

import jax
import jax.numpy as jnp
from jax import lax
from jax.experimental import pallas as pl
from jax.experimental.pallas import tpu as pltpu
from jax.sharding import PartitionSpec as P

DEGREE = 4
LEVELS = 3
SPLIT = 2
BOTTOM_ITERS = 20
LANES = 128

smooth_low = 1.5
smooth_top = 12.0
absorb_top = 1.0
bottom_low = 0.008

MESH = pl.DeviceIdType.MESH
AXES = ("gx", "gz", "gy")


def cheb_tables(count, lower, upper):
    theta = (upper + lower) / 2.0
    delta = (upper - lower) / 2.0
    sigma = theta / delta
    rho_value = 1.0 / sigma
    firsts = []
    seconds = []
    for turn_index in range(count - 1):
        rho_next = 1.0 / (2.0 * sigma - rho_value)
        firsts.append(rho_next * rho_value)
        seconds.append(2.0 * rho_next / delta)
        rho_value = rho_next
    return (1.0 / theta, firsts, seconds)


def exact_dot(left, right):
    return jnp.dot(
        left, right, precision=lax.Precision.HIGHEST, preferred_element_type=jnp.float32
    )


def lanes_of(shape):
    return lax.broadcasted_iota(jnp.int32, shape, len(shape) - 1)


def rows_of(shape):
    return lax.broadcasted_iota(jnp.int32, shape, len(shape) - 2)


def halving():
    j = rows_of((LANES, LANES))
    i = lanes_of((LANES, LANES))
    return jnp.where(j // 2 == i, jnp.float32(0.5), jnp.float32(0.0))


def trilinear(coarse, fine):
    centre = fine // 2
    other = centre + 2 * (fine % 2) - 1
    return jnp.where(coarse == centre, jnp.float32(0.75), jnp.float32(0.0)) + jnp.where(
        coarse == other, jnp.float32(0.25), jnp.float32(0.0)
    )


def kernel(sizes, blocks, rs_hbm, ab_hbm, out0, out1, out2, *scratch):
    nx, nz, ny = sizes
    me = {a: lax.axis_index(a) for a in AXES}
    count = dict(zip(AXES, sizes))
    has_lo = {a: me[a] > 0 for a in AXES}
    has_hi = {a: me[a] < count[a] - 1 for a in AXES}

    per_level = 9
    level_refs = [list(scratch[per_level * k : per_level * (k + 1)]) for k in range(SPLIT)]
    level_refs[0][7] = out0
    rest = scratch[per_level * SPLIT :]
    rs, ab, pairs, gath_s, gath_c, src2, coef2, dir2, res2, it2 = rest[:10]
    src3, coef3, dir3, res3, it3, tab = rest[10:16]
    send_sem, recv_sem, gsend, grecv, fetch_sem = rest[16:]

    fetches = [
        pltpu.make_async_copy(rs_hbm, rs, fetch_sem.at[0]),
        pltpu.make_async_copy(ab_hbm, ab, fetch_sem.at[1]),
    ]
    for fetch in fetches:
        fetch.start()

    bottom_scale, firsts, seconds = cheb_tables(
        BOTTOM_ITERS, bottom_low, smooth_top + 4.0**LEVELS * absorb_top
    )
    for n in range(BOTTOM_ITERS - 1):
        tab[0, n] = jnp.float32(firsts[n])
        tab[1, n] = jnp.float32(seconds[n])

    barrier = pltpu.get_barrier_semaphore()
    greeted = 0
    for a in AXES:
        for k in range(1, count[a]):
            pl.semaphore_signal(
                barrier,
                inc=1,
                device_id={a: lax.rem(me[a] + k, count[a])},
                device_id_type=MESH,
            )
            greeted += 1
    pl.semaphore_wait(barrier, greeted)

    half = halving()

    def restrict(read, shape):
        first, second, _ = shape
        for x in range(first // 2):
            pairs[pl.ds(x * second, second), :] = read(2 * x) + read(2 * x + 1)
        total = first // 2 * second // 2
        summed = (
            pairs[pl.ds(0, total, stride=2), :] + pairs[pl.ds(1, total, stride=2), :]
        )
        return exact_dot(summed, half)

    def copies(level, r):
        first, second, _ = blocks[level]
        dirs, faces_z, faces_y, halo_x, halo_z, halo_y = level_refs[level][:6]
        slot = level * (DEGREE + 1) + r
        ends = {
            "gx": (dirs.at[r, 1], dirs.at[r, first], halo_x),
            "gz": (faces_z.at[r, 0], faces_z.at[r, 1], halo_z),
            "gy": (faces_y.at[r], faces_y.at[r], halo_y),
        }
        made = []
        for n, a in enumerate(AXES):
            low_face, high_face, halo = ends[a]
            made.append(
                (
                    has_lo[a],
                    has_hi[a],
                    pltpu.make_async_remote_copy(
                        src_ref=low_face,
                        dst_ref=halo.at[r, 1],
                        send_sem=send_sem.at[slot, 2 * n],
                        recv_sem=recv_sem.at[slot, 2 * n],
                        device_id={a: jnp.maximum(me[a] - 1, 0)},
                        device_id_type=MESH,
                    ),
                )
            )
            made.append(
                (
                    has_hi[a],
                    has_lo[a],
                    pltpu.make_async_remote_copy(
                        src_ref=high_face,
                        dst_ref=halo.at[r, 0],
                        send_sem=send_sem.at[slot, 2 * n + 1],
                        recv_sem=recv_sem.at[slot, 2 * n + 1],
                        device_id={a: jnp.minimum(me[a] + 1, count[a] - 1)},
                        device_id_type=MESH,
                    ),
                )
            )
        return made

    def start(level, r):
        for sends, _, copy in copies(level, r):
            pl.when(sends)(copy.start)

    def arrive(level, r):
        for _, gets, copy in copies(level, r):
            pl.when(gets)(copy.wait_recv)

    def sent(level, r):
        for sends, _, copy in copies(level, r):
            pl.when(sends)(copy.wait_send)

    def put_faces(level, r, x, field, packed):
        second, width = blocks[level][1:]
        dirs, faces_z = level_refs[level][:2]
        dirs[r, x + 1] = field
        faces_z[r, 0, pl.ds(x, 1), :] = field[:1]
        faces_z[r, 1, pl.ds(x, 1), :] = field[second - 1 :]
        lane = lanes_of((second, LANES))
        low = pltpu.roll(field, 2 * x + 1, 1)
        if width == LANES:
            return jnp.where(lane // 2 == x, low, packed)
        high = pltpu.roll(field, 2 * x + LANES + 1 - width, 1)
        return jnp.where(lane == 2 * x + 1, low, jnp.where(lane == 2 * x, high, packed))

    def by_chunks(level, body, carry):
        first, second, _ = blocks[level]
        chunk = min(first, 256 // second)

        def turn(n, carry):
            return body([n * chunk + j for j in range(chunk)], carry)

        if chunk == first:
            return turn(0, carry)
        return lax.fori_loop(0, first // chunk, turn, carry)

    edge_row = rows_of((8, LANES))

    def inside(level, r, base, coef):
        first, second, width = blocks[level]
        dirs = level_refs[level][0]
        resid = level_refs[level][6]
        lane = lanes_of((second, LANES))

        def body(xs, carry):
            layers = [dirs[r, xs[0] + j] for j in range(len(xs) + 2)]
            bases = [base[x] for x in xs]
            parts = [coef[x] for x in xs]
            results = []
            for j in range(len(xs)):
                d = layers[j + 1]
                near = layers[j] + layers[j + 2]
                up = pltpu.roll(d, 1, 0)
                down = pltpu.roll(d, second - 1, 0)
                up = jnp.concatenate((jnp.where(edge_row == 0, 0.0, up[:8]), up[8:]), 0)
                down = jnp.concatenate(
                    (down[: second - 8], jnp.where(edge_row == 7, 0.0, down[second - 8 :])), 0
                )
                near += up + down
                near += pltpu.roll(d, 1, 1) + pltpu.roll(d, LANES - 1, 1)
                if width < LANES:
                    near = jnp.where(lane < width, near, 0.0)
                results.append(bases[j] - ((6.0 + parts[j]) * d - near))
            for j, x in enumerate(xs):
                resid[x] = results[j]
            return carry

        by_chunks(level, body, 0)

    def outside(level, r):
        first, second, width = blocks[level]
        faces_y, halo_x, halo_z, halo_y = level_refs[level][2:6]
        resid = level_refs[level][6]
        lane = lanes_of((second, LANES))
        resid[0] += jnp.where(has_lo["gx"], halo_x[r, 0], 0.0)
        resid[first - 1] += jnp.where(has_hi["gx"], halo_x[r, 1], 0.0)
        low = jnp.where(has_lo["gy"], halo_y[r, 0], 0.0)
        high = jnp.where(has_hi["gy"], halo_y[r, 1], 0.0)
        if width == LANES:
            low -= faces_y[r]
            high -= faces_y[r]
        ends = jnp.where(lane % 2 == 1, pltpu.roll(low, 1, 1), pltpu.roll(high, LANES - 1, 1))

        def add(x):
            res = resid[x]
            z_low = jnp.where(has_lo["gz"], halo_z[r, 0, pl.ds(x, 1), :], 0.0)
            z_high = jnp.where(has_hi["gz"], halo_z[r, 1, pl.ds(x, 1), :], 0.0)
            res = jnp.concatenate(
                (
                    res[:8] + jnp.where(edge_row == 0, z_low, 0.0),
                    res[8 : second - 8],
                    res[second - 8 :] + jnp.where(edge_row == 7, z_high, 0.0),
                )[:: 1 if second > 16 else 2],
                0,
            )
            to_low = pltpu.roll(ends, LANES - 1 - 2 * x, 1)
            if width == LANES:
                res += jnp.where((lane == 0) | (lane == LANES - 1), to_low, 0.0)
            else:
                to_high = pltpu.roll(ends, width - 1 - 2 * x, 1)
                res += jnp.where(lane == 0, to_low, jnp.where(lane == width - 1, to_high, 0.0))
            return res

        return add

    def smooth(level, source, coef, between):
        first, second, width = blocks[level]
        dirs, _, faces_y = level_refs[level][:3]
        resid, iterate = level_refs[level][6:8]
        upper = smooth_top + 4.0**level * absorb_top
        scale, firsts, seconds = cheb_tables(DEGREE + 1, smooth_low, upper)
        empty = jnp.zeros((second, LANES), jnp.float32)
        for r in range(DEGREE + 1):
            dirs[r, 0] = empty
            dirs[r, first + 1] = empty

        def opening(xs, packed):
            fields = [source[x] * scale for x in xs]
            for x, d in zip(xs, fields):
                iterate[x] = d
                packed = put_faces(level, 0, x, d, packed)
            return packed

        faces_y[0] = by_chunks(level, opening, empty)
        for r in range(DEGREE + 1):
            start(level, r)
            if level == 0 and r == 0:
                fetches[1].wait()
            inside(level, r, source if r in (0, DEGREE) else resid, coef)
            if r in between:
                between[r]()
            arrive(level, r)
            add = outside(level, r)

            def last(xs, carry, add=add):
                results = [add(x) for x in xs]
                for x, res in zip(xs, results):
                    resid[x] = res
                return carry

            def turn(xs, packed, r=r, add=add):
                results = [add(x) for x in xs]
                fields = [
                    firsts[r] * dirs[r, x + 1] + seconds[r] * res for x, res in zip(xs, results)
                ]
                totals = [iterate[x] + d for x, d in zip(xs, fields)]
                for x, res, d, total in zip(xs, results, fields, totals):
                    resid[x] = res
                    iterate[x] = total
                    packed = put_faces(
                        level, r + 1, x, total if r == DEGREE - 1 else d, packed
                    )
                return packed

            if r == DEGREE:
                by_chunks(level, last, 0)
            else:
                faces_y[r + 1] = by_chunks(level, turn, empty)

    coef1, source1 = level_refs[1][8].at[0], level_refs[1][8].at[1]
    first2, second2, width2 = blocks[2]
    whole2 = (first2 * nx, second2 * nz, width2 * ny)
    whole3 = tuple(s // 2 for s in whole2)

    def spread(rows, shape, ref):
        for x in range(shape[0]):
            ref[x] = rows[x * shape[1] : (x + 1) * shape[1]]

    def into_message(rows):
        packed = rows[:second2]
        for x in range(1, first2):
            packed += pltpu.roll(rows[x * second2 : (x + 1) * second2], x * width2, 1)
        return packed

    def line(a, which, gath):
        piece = {
            "gz": gath.at[me["gx"], me["gy"], me["gz"]],
            "gx": gath.at[me["gx"], me["gy"]],
            "gy": gath.at[:, me["gy"]],
        }[a]
        base = {"gz": 0, "gx": nz - 1, "gy": nz + nx - 2}[a]
        return [
            pltpu.make_async_remote_copy(
                src_ref=piece,
                dst_ref=piece,
                send_sem=gsend.at[which, base + k - 1],
                recv_sem=grecv.at[which, base + k - 1],
                device_id={a: lax.rem(me[a] + k, count[a])},
                device_id_type=MESH,
            )
            for k in range(1, count[a])
        ]

    def begin(copies):
        for copy in copies:
            copy.start()

    def finish(copies):
        for copy in copies:
            copy.wait_recv()
        for copy in copies:
            copy.wait_send()

    def place(gath, ref):
        lane = lanes_of((second2, LANES))

        @pl.loop(0, nx * nz // 2)
        def _(n):
            for m in (2 * n, 2 * n + 1):
                ix = m // nz
                iz = m % nz
                held = [gath[ix, iy, iz] for iy in range(ny)]
                for x in range(first2):
                    tile = jnp.zeros((second2, LANES), jnp.float32)
                    for iy in range(ny):
                        shift = (iy - x) * width2 % LANES
                        moved = pltpu.roll(held[iy], shift, 1) if shift else held[iy]
                        tile = jnp.where(lane // width2 == iy, moved, tile)
                    start_row = pl.multiple_of(iz * second2, second2)
                    ref[ix * first2 + x, pl.ds(start_row, second2), :] = tile

    def coarsen():
        spread(restrict(lambda x: ab[x], blocks[0]), blocks[1], coef1)
        rows = restrict(lambda x: coef1[x], blocks[1])
        gath_c[me["gx"], me["gy"], me["gz"]] = into_message(rows)
        begin(line("gz", 0, gath_c))

    def coarse_x():
        finish(line("gz", 0, gath_c))
        begin(line("gx", 0, gath_c))

    def coarse_y():
        finish(line("gx", 0, gath_c))
        begin(line("gy", 0, gath_c))

    def coarse_all():
        finish(line("gy", 0, gath_c))
        place(gath_c, coef2)

    def coarse_bottom():
        spread(restrict(lambda x: coef2[x], whole2), whole3, coef3)

    fetches[0].wait()
    smooth(0, rs, ab, {0: coarsen, 1: coarse_x, 2: coarse_y})
    resid = level_refs[0][6]
    spread(restrict(lambda x: resid[x], blocks[0]), blocks[1], source1)
    smooth(1, source1, coef1, {0: coarse_all, 1: coarse_bottom})
    rows = restrict(lambda x: level_refs[1][6][x], blocks[1])

    gath_s[me["gx"], me["gy"], me["gz"]] = into_message(rows)
    for a in ("gz", "gx", "gy"):
        begin(line(a, 1, gath_s))
        if a == "gz":
            width1 = blocks[1][2]
            for x in range(blocks[1][0]):
                out1[x] = level_refs[1][7][x][:, :width1]
        finish(line(a, 1, gath_s))
    place(gath_s, src2)

    def neighbour_sum(below, d, above, width):
        second = d.shape[0]
        lane = lanes_of(d.shape)
        near = below + above
        up = pltpu.roll(d, 1, 0)
        down = pltpu.roll(d, second - 1, 0)
        up = jnp.concatenate((jnp.where(edge_row == 0, 0.0, up[:8]), up[8:]), 0)
        down = jnp.concatenate(
            (down[: second - 8], jnp.where(edge_row == 7, 0.0, down[second - 8 :])), 0
        )
        near += up + down
        left = pltpu.roll(d, 1, 1)
        right = pltpu.roll(d, LANES - 1, 1)
        if width == LANES:
            near += jnp.where(lane == 0, 0.0, left) + jnp.where(lane == LANES - 1, 0.0, right)
            return near
        return jnp.where(lane < width, near + left + right, 0.0)

    total_x, total_z, total_y = whole2
    zero = jnp.zeros((total_z, LANES), jnp.float32)
    scale, firsts, seconds = cheb_tables(
        DEGREE + 1, smooth_low, smooth_top + 4.0 ** (LEVELS - 1) * absorb_top
    )
    for slot in range(2):
        dir2[slot, 0] = zero
        dir2[slot, total_x + 1] = zero
    chunk = max(1, min(total_x, 256 // total_z))

    @pl.loop(0, total_x // chunk)
    def _(n):
        fields = [src2[n * chunk + j] * scale for j in range(chunk)]
        for j in range(chunk):
            dir2[0, n * chunk + j + 1] = fields[j]
            it2[n * chunk + j] = fields[j]

    for r in range(DEGREE + 1):
        old, new = r % 2, (r + 1) % 2

        @pl.loop(0, total_x // chunk)
        def _(n, r=r, old=old, new=new):
            xs = [n * chunk + j for j in range(chunk)]
            layers = [dir2[old, xs[0] + j] for j in range(chunk + 2)]
            bases = [(src2 if r in (0, DEGREE) else res2)[x] for x in xs]
            parts = [coef2[x] for x in xs]
            results = []
            for j in range(chunk):
                near = neighbour_sum(layers[j], layers[j + 1], layers[j + 2], total_y)
                results.append(bases[j] - ((6.0 + parts[j]) * layers[j + 1] - near))
            if r < DEGREE:
                fields = [
                    firsts[r] * layers[j + 1] + seconds[r] * results[j] for j in range(chunk)
                ]
                totals = [it2[x] + d for x, d in zip(xs, fields)]
                for j, x in enumerate(xs):
                    it2[x] = totals[j]
                    dir2[new, x + 1] = totals[j] if r == DEGREE - 1 else fields[j]
            for j, x in enumerate(xs):
                res2[x] = results[j]

    spread(restrict(lambda x: res2[x], whole2), whole3, src3)

    whole_x, whole_z, whole_y = whole3
    zero = jnp.zeros((whole_z, LANES), jnp.float32)
    for ref in (dir3, it3):
        ref[0] = zero
        ref[whole_x + 1] = zero
    for x in range(whole_x):
        source = src3[x]
        res3[x] = source
        dir3[x + 1] = source * bottom_scale
        it3[x + 1] = source * bottom_scale

    def bottom_turn(n, carry):
        one = tab[0, n]
        two = tab[1, n]
        layers = [dir3[x] for x in range(whole_x + 2)]
        bases = [res3[x] for x in range(whole_x)]
        for x in range(whole_x):
            near = neighbour_sum(layers[x], layers[x + 1], layers[x + 2], whole_y)
            res = bases[x] - ((6.0 + coef3[x]) * layers[x + 1] - near)
            d = one * layers[x + 1] + two * res
            res3[x] = res
            dir3[x + 1] = d
            it3[x + 1] += d
        return carry

    lax.fori_loop(0, BOTTOM_ITERS - 1, bottom_turn, 0)

    i = lanes_of((LANES, LANES))
    along_y = jnp.where(
        i < width2, trilinear(rows_of((LANES, LANES)), me["gy"] * width2 + i), 0.0
    )
    along_z = trilinear(
        lanes_of((second2, whole_z)), me["gz"] * second2 + rows_of((second2, whole_z))
    )
    layers = []
    for x in range(first2):
        centre = me["gx"] * (first2 // 2) + x // 2 + 1
        layers.append(0.75 * it3[centre] + 0.25 * it3[centre + 2 * (x % 2) - 1])
    moved = exact_dot(jnp.concatenate(layers, axis=0), along_y)
    own_rows = pl.ds(pl.multiple_of(me["gz"] * second2, second2), second2)
    back = lax.rem(LANES - me["gy"] * width2, LANES)
    for x in range(first2):
        fine = exact_dot(along_z, moved[x * whole_z : (x + 1) * whole_z])
        own = pltpu.roll(it2[me["gx"] * first2 + x, own_rows, :], back, 1)
        out2[x] = (own + fine)[:, :width2]

    for level in range(SPLIT):
        for r in range(DEGREE + 1):
            sent(level, r)


def on_device(sizes, right_side, absorption):
    nx, nz, ny = sizes
    blocks = [tuple(s // 2**k for s in right_side.shape) for k in range(LEVELS)]
    rounds = DEGREE + 1
    scratch = []
    for first, second, width in blocks[:SPLIT]:
        scratch += [
            pltpu.VMEM((rounds, first + 2, second, LANES), jnp.float32),
            pltpu.VMEM((rounds, 2, first, LANES), jnp.float32),
            pltpu.VMEM((rounds, second, LANES), jnp.float32),
            pltpu.VMEM((rounds, 2, second, LANES), jnp.float32),
            pltpu.VMEM((rounds, 2, first, LANES), jnp.float32),
            pltpu.VMEM((rounds, 2, second, LANES), jnp.float32),
            pltpu.VMEM((first, second, LANES), jnp.float32),
            pltpu.VMEM((first, second, LANES), jnp.float32),
            pltpu.VMEM((2, first, second, LANES), jnp.float32),
        ]
    first2, second2, _ = blocks[2]
    x2, z2 = first2 * nx, second2 * nz
    x3, z3 = x2 // 2, z2 // 2
    pair_rows = max(blocks[0][0] // 2 * blocks[0][1], x2 // 2 * z2)
    lines = nx + ny + nz - 3
    scratch += [
        pltpu.VMEM(right_side.shape, jnp.float32),
        pltpu.VMEM(right_side.shape, jnp.float32),
        pltpu.VMEM((pair_rows, LANES), jnp.float32),
        pltpu.VMEM((nx, ny, nz, second2, LANES), jnp.float32),
        pltpu.VMEM((nx, ny, nz, second2, LANES), jnp.float32),
        pltpu.VMEM((x2, z2, LANES), jnp.float32),
        pltpu.VMEM((x2, z2, LANES), jnp.float32),
        pltpu.VMEM((2, x2 + 2, z2, LANES), jnp.float32),
        pltpu.VMEM((x2, z2, LANES), jnp.float32),
        pltpu.VMEM((x2, z2, LANES), jnp.float32),
        pltpu.VMEM((x3, z3, LANES), jnp.float32),
        pltpu.VMEM((x3, z3, LANES), jnp.float32),
        pltpu.VMEM((x3 + 2, z3, LANES), jnp.float32),
        pltpu.VMEM((x3, z3, LANES), jnp.float32),
        pltpu.VMEM((x3 + 2, z3, LANES), jnp.float32),
        pltpu.SMEM((2, BOTTOM_ITERS - 1), jnp.float32),
        pltpu.SemaphoreType.DMA((SPLIT * rounds, 6)),
        pltpu.SemaphoreType.DMA((SPLIT * rounds, 6)),
        pltpu.SemaphoreType.DMA((2, lines)),
        pltpu.SemaphoreType.DMA((2, lines)),
        pltpu.SemaphoreType.DMA((2,)),
    ]
    vmem = pl.BlockSpec(memory_space=pltpu.VMEM)
    return pl.pallas_call(
        functools.partial(kernel, sizes, blocks),
        out_shape=tuple(jax.ShapeDtypeStruct(b, jnp.float32) for b in blocks),
        in_specs=[pl.BlockSpec(memory_space=pl.ANY)] * 2,
        out_specs=(vmem, vmem, vmem),
        scratch_shapes=scratch,
        compiler_params=pltpu.CompilerParams(
            collective_id=0, has_side_effects=True, vmem_limit_bytes=48 * 1024 * 1024
        ),
    )(right_side, absorption)


def solution(mesh):
    sizes = tuple(mesh.shape[a] for a in AXES)
    spec = P("gx", "gz", "gy")
    return jax.shard_map(
        functools.partial(on_device, sizes),
        mesh=mesh,
        in_specs=(spec, spec),
        out_specs=(spec, spec, spec),
        check_vma=False,
    )
```

```python
import functools

import jax
import jax.numpy as jnp
from jax import lax
from jax.experimental import pallas as pl
from jax.experimental.pallas import tpu as pltpu
from jax.sharding import PartitionSpec as P

DEGREE = 4
LEVELS = 3
SPLIT = 2
BOTTOM_ITERS = 20
LANES = 128

smooth_low = 1.5
smooth_top = 12.0
absorb_top = 1.0
bottom_low = 0.008

MESH = pl.DeviceIdType.MESH
AXES = ("gx", "gz", "gy")


def cheb_tables(count, lower, upper):
    theta = (upper + lower) / 2.0
    delta = (upper - lower) / 2.0
    sigma = theta / delta
    rho_value = 1.0 / sigma
    firsts = []
    seconds = []
    for turn_index in range(count - 1):
        rho_next = 1.0 / (2.0 * sigma - rho_value)
        firsts.append(rho_next * rho_value)
        seconds.append(2.0 * rho_next / delta)
        rho_value = rho_next
    return (1.0 / theta, firsts, seconds)


def exact_dot(left, right):
    return jnp.dot(
        left, right, precision=lax.Precision.HIGHEST, preferred_element_type=jnp.float32
    )


def lanes_of(shape):
    return lax.broadcasted_iota(jnp.int32, shape, len(shape) - 1)


def rows_of(shape):
    return lax.broadcasted_iota(jnp.int32, shape, len(shape) - 2)


def halving():
    j = rows_of((LANES, LANES))
    i = lanes_of((LANES, LANES))
    return jnp.where(j // 2 == i, jnp.float32(0.5), jnp.float32(0.0))


def trilinear(coarse, fine):
    centre = fine // 2
    other = centre + 2 * (fine % 2) - 1
    return jnp.where(coarse == centre, jnp.float32(0.75), jnp.float32(0.0)) + jnp.where(
        coarse == other, jnp.float32(0.25), jnp.float32(0.0)
    )


def kernel(sizes, blocks, rs_hbm, ab_hbm, out0, out1, out2, *scratch):
    nx, nz, ny = sizes
    me = {a: lax.axis_index(a) for a in AXES}
    count = dict(zip(AXES, sizes))
    has_lo = {a: me[a] > 0 for a in AXES}
    has_hi = {a: me[a] < count[a] - 1 for a in AXES}

    per_level = 9
    level_refs = [list(scratch[per_level * k : per_level * (k + 1)]) for k in range(SPLIT)]
    level_refs[0][7] = out0
    rest = scratch[per_level * SPLIT :]
    rs, ab, pairs, gath_s, gath_c, src2, coef2, dir2, res2, it2 = rest[:10]
    src3, coef3, dir3, res3, it3, tab = rest[10:16]
    send_sem, recv_sem, gsend, grecv, fetch_sem = rest[16:]

    fetches = [
        pltpu.make_async_copy(rs_hbm, rs, fetch_sem.at[0]),
        pltpu.make_async_copy(ab_hbm, ab, fetch_sem.at[1]),
    ]
    for fetch in fetches:
        fetch.start()

    bottom_scale, firsts, seconds = cheb_tables(
        BOTTOM_ITERS, bottom_low, smooth_top + 4.0**LEVELS * absorb_top
    )
    for n in range(BOTTOM_ITERS - 1):
        tab[0, n] = jnp.float32(firsts[n])
        tab[1, n] = jnp.float32(seconds[n])

    z_peers = [{"gz": k} for k in range(1, nz)]
    plane_peers = [
        {"gx": i, "gy": j} for i in range(nx) for j in range(ny) if (i, j) != (0, 0)
    ]

    def device(offsets):
        return {a: lax.rem(me[a] + k, count[a]) for a, k in offsets.items()}

    barrier = pltpu.get_barrier_semaphore()
    for peer in z_peers + plane_peers:
        pl.semaphore_signal(barrier, inc=1, device_id=device(peer), device_id_type=MESH)

    half = halving()

    def restrict(read, shape):
        first, second, _ = shape
        for x in range(first // 2):
            pairs[pl.ds(x * second, second), :] = read(2 * x) + read(2 * x + 1)
        total = first // 2 * second // 2
        summed = (
            pairs[pl.ds(0, total, stride=2), :] + pairs[pl.ds(1, total, stride=2), :]
        )
        return exact_dot(summed, half)

    def copies(level, r):
        first, second, _ = blocks[level]
        dirs, faces_z, faces_y, halo_x, halo_z, halo_y = level_refs[level][:6]
        slot = level * (DEGREE + 1) + r
        ends = {
            "gx": (dirs.at[r, 1], dirs.at[r, first], halo_x),
            "gz": (faces_z.at[r, 0], faces_z.at[r, 1], halo_z),
            "gy": (faces_y.at[r], faces_y.at[r], halo_y),
        }
        made = []
        for n, a in enumerate(AXES):
            low_face, high_face, halo = ends[a]
            made.append(
                (
                    has_lo[a],
                    has_hi[a],
                    pltpu.make_async_remote_copy(
                        src_ref=low_face,
                        dst_ref=halo.at[r, 1],
                        send_sem=send_sem.at[slot, 2 * n],
                        recv_sem=recv_sem.at[slot, 2 * n],
                        device_id={a: jnp.maximum(me[a] - 1, 0)},
                        device_id_type=MESH,
                    ),
                )
            )
            made.append(
                (
                    has_hi[a],
                    has_lo[a],
                    pltpu.make_async_remote_copy(
                        src_ref=high_face,
                        dst_ref=halo.at[r, 0],
                        send_sem=send_sem.at[slot, 2 * n + 1],
                        recv_sem=recv_sem.at[slot, 2 * n + 1],
                        device_id={a: jnp.minimum(me[a] + 1, count[a] - 1)},
                        device_id_type=MESH,
                    ),
                )
            )
        return made

    def start(level, r, part):
        for sends, _, copy in copies(level, r)[part]:
            pl.when(sends)(copy.start)

    along_x, along_zy = slice(0, 2), slice(2, 6)

    def arrive(level, r):
        for _, gets, copy in copies(level, r):
            pl.when(gets)(copy.wait_recv)

    def all_sent():
        rounds = [copies(level, r) for level in range(SPLIT) for r in range(DEGREE + 1)]
        for way in range(6):

            @pl.when(rounds[0][way][0])
            def _(way=way):
                for made in rounds:
                    made[way][2].wait_send()

    def put_faces(level, r, x, field, packed):
        second, width = blocks[level][1:]
        dirs, faces_z = level_refs[level][:2]
        dirs[r, x + 1] = field
        faces_z[r, 0, pl.ds(x, 1), :] = field[:1]
        faces_z[r, 1, pl.ds(x, 1), :] = field[second - 1 :]
        lane = lanes_of((second, LANES))
        low = pltpu.roll(field, 2 * x + 1, 1)
        if width == LANES:
            return jnp.where(lane // 2 == x, low, packed)
        high = pltpu.roll(field, 2 * x + LANES + 1 - width, 1)
        return jnp.where(lane == 2 * x + 1, low, jnp.where(lane == 2 * x, high, packed))

    def by_chunks(level, body, carry, ends_done=None):
        first, second, _ = blocks[level]
        chunk = min(first, 256 // second)
        turns = first // chunk

        def turn(n, carry):
            if turns > 2:
                chosen = jnp.where(n == 0, 0, jnp.where(n == 1, turns - 1, n - 1))
            else:
                chosen = n
            carry = body([chosen * chunk + j for j in range(chunk)], carry)
            if ends_done is not None and turns > 1:
                pl.when(n == 1)(ends_done)
            return carry

        if turns == 1:
            carry = turn(0, carry)
            if ends_done is not None:
                ends_done()
            return carry
        return lax.fori_loop(0, turns, turn, carry)

    edge_row = rows_of((8, LANES))

    def inside(level, r, base, coef):
        first, second, width = blocks[level]
        dirs = level_refs[level][0]
        resid = level_refs[level][6]
        lane = lanes_of((second, LANES))

        def body(xs, carry):
            layers = [dirs[r, xs[0] + j] for j in range(len(xs) + 2)]
            bases = [base[x] for x in xs]
            parts = [coef[x] for x in xs]
            results = []
            for j in range(len(xs)):
                d = layers[j + 1]
                near = layers[j] + layers[j + 2]
                up = pltpu.roll(d, 1, 0)
                down = pltpu.roll(d, second - 1, 0)
                up = jnp.concatenate((jnp.where(edge_row == 0, 0.0, up[:8]), up[8:]), 0)
                down = jnp.concatenate(
                    (down[: second - 8], jnp.where(edge_row == 7, 0.0, down[second - 8 :])), 0
                )
                near += up + down
                near += pltpu.roll(d, 1, 1) + pltpu.roll(d, LANES - 1, 1)
                if width < LANES:
                    near = jnp.where(lane < width, near, 0.0)
                results.append(bases[j] - ((6.0 + parts[j]) * d - near))
            for j, x in enumerate(xs):
                resid[x] = results[j]
            return carry

        by_chunks(level, body, 0)

    def outside(level, r):
        first, second, width = blocks[level]
        faces_y, halo_x, halo_z, halo_y = level_refs[level][2:6]
        resid = level_refs[level][6]
        lane = lanes_of((second, LANES))
        resid[0] += jnp.where(has_lo["gx"], halo_x[r, 0], 0.0)
        resid[first - 1] += jnp.where(has_hi["gx"], halo_x[r, 1], 0.0)
        low = jnp.where(has_lo["gy"], halo_y[r, 0], 0.0)
        high = jnp.where(has_hi["gy"], halo_y[r, 1], 0.0)
        if width == LANES:
            low -= faces_y[r]
            high -= faces_y[r]
        ends = jnp.where(lane % 2 == 1, pltpu.roll(low, 1, 1), pltpu.roll(high, LANES - 1, 1))

        def add(x):
            res = resid[x]
            z_low = jnp.where(has_lo["gz"], halo_z[r, 0, pl.ds(x, 1), :], 0.0)
            z_high = jnp.where(has_hi["gz"], halo_z[r, 1, pl.ds(x, 1), :], 0.0)
            res = jnp.concatenate(
                (
                    res[:8] + jnp.where(edge_row == 0, z_low, 0.0),
                    res[8 : second - 8],
                    res[second - 8 :] + jnp.where(edge_row == 7, z_high, 0.0),
                )[:: 1 if second > 16 else 2],
                0,
            )
            to_low = pltpu.roll(ends, LANES - 1 - 2 * x, 1)
            if width == LANES:
                res += jnp.where((lane == 0) | (lane == LANES - 1), to_low, 0.0)
            else:
                to_high = pltpu.roll(ends, width - 1 - 2 * x, 1)
                res += jnp.where(lane == 0, to_low, jnp.where(lane == width - 1, to_high, 0.0))
            return res

        return add

    def smooth(level, source, coef, between):
        first, second, width = blocks[level]
        dirs, _, faces_y = level_refs[level][:3]
        resid, iterate = level_refs[level][6:8]
        upper = smooth_top + 4.0**level * absorb_top
        scale, firsts, seconds = cheb_tables(DEGREE + 1, smooth_low, upper)
        empty = jnp.zeros((second, LANES), jnp.float32)
        for r in range(DEGREE + 1):
            dirs[r, 0] = empty
            dirs[r, first + 1] = empty

        def opening(xs, packed):
            fields = [source[x] * scale for x in xs]
            for x, d in zip(xs, fields):
                iterate[x] = d
                packed = put_faces(level, 0, x, d, packed)
            return packed

        faces_y[0] = by_chunks(level, opening, empty)
        if level == 0:
            pl.semaphore_wait(barrier, len(z_peers) + len(plane_peers))
        start(level, 0, along_x)
        for r in range(DEGREE + 1):
            start(level, r, along_zy)
            if level == 0 and r == 0:
                fetches[1].wait()
            inside(level, r, source if r in (0, DEGREE) else resid, coef)
            if r in between:
                between[r]()
            arrive(level, r)
            add = outside(level, r)

            def last(xs, carry, add=add):
                results = [add(x) for x in xs]
                for x, res in zip(xs, results):
                    resid[x] = res
                return carry

            def turn(xs, packed, r=r, add=add):
                results = [add(x) for x in xs]
                fields = [
                    firsts[r] * dirs[r, x + 1] + seconds[r] * res for x, res in zip(xs, results)
                ]
                totals = [iterate[x] + d for x, d in zip(xs, fields)]
                for x, res, d, total in zip(xs, results, fields, totals):
                    resid[x] = res
                    iterate[x] = total
                    packed = put_faces(
                        level, r + 1, x, total if r == DEGREE - 1 else d, packed
                    )
                return packed

            if r == DEGREE:
                by_chunks(level, last, 0)
            else:
                faces_y[r + 1] = by_chunks(
                    level, turn, empty, lambda r=r: start(level, r + 1, along_x)
                )

    coef1, source1 = level_refs[1][8].at[0], level_refs[1][8].at[1]
    first2, second2, width2 = blocks[2]
    whole2 = (first2 * nx, second2 * nz, width2 * ny)
    whole3 = tuple(s // 2 for s in whole2)

    def spread(rows, shape, ref):
        for x in range(shape[0]):
            ref[x] = rows[x * shape[1] : (x + 1) * shape[1]]

    def into_message(rows):
        packed = rows[:second2]
        for x in range(1, first2):
            packed += pltpu.roll(rows[x * second2 : (x + 1) * second2], x * width2, 1)
        return packed

    def line(which, gath):
        piece = gath.at[me["gx"], me["gy"], me["gz"]]
        return gather(piece, which, z_peers, 0)

    def plane(which, gath):
        piece = gath.at[me["gx"], me["gy"]]
        return gather(piece, which, plane_peers, len(z_peers))

    def gather(piece, which, peers, base):
        return [
            pltpu.make_async_remote_copy(
                src_ref=piece,
                dst_ref=piece,
                send_sem=gsend.at[which, base + k],
                recv_sem=grecv.at[which, base + k],
                device_id=device(peer),
                device_id_type=MESH,
            )
            for k, peer in enumerate(peers)
        ]

    def begin(copies):
        for copy in copies:
            copy.start()

    def finish(copies):
        for copy in copies:
            copy.wait_recv()
        for copy in copies:
            copy.wait_send()

    def place(gath, ref):
        lane = lanes_of((second2, LANES))

        @pl.loop(0, nx * nz // 2)
        def _(n):
            for m in (2 * n, 2 * n + 1):
                ix = m // nz
                iz = m % nz
                held = [gath[ix, iy, iz] for iy in range(ny)]
                for x in range(first2):
                    tile = jnp.zeros((second2, LANES), jnp.float32)
                    for iy in range(ny):
                        shift = (iy - x) * width2 % LANES
                        moved = pltpu.roll(held[iy], shift, 1) if shift else held[iy]
                        tile = jnp.where(lane // width2 == iy, moved, tile)
                    start_row = pl.multiple_of(iz * second2, second2)
                    ref[ix * first2 + x, pl.ds(start_row, second2), :] = tile

    def coarsen():
        spread(restrict(lambda x: ab[x], blocks[0]), blocks[1], coef1)
        rows = restrict(lambda x: coef1[x], blocks[1])
        gath_c[me["gx"], me["gy"], me["gz"]] = into_message(rows)
        begin(line(0, gath_c))

    def coarse_plane():
        finish(line(0, gath_c))
        begin(plane(0, gath_c))

    def coarse_all():
        finish(plane(0, gath_c))
        place(gath_c, coef2)

    def coarse_bottom():
        spread(restrict(lambda x: coef2[x], whole2), whole3, coef3)

    fetches[0].wait()
    smooth(0, rs, ab, {0: coarsen})
    resid = level_refs[0][6]
    spread(restrict(lambda x: resid[x], blocks[0]), blocks[1], source1)
    smooth(1, source1, coef1, {0: coarse_plane, 3: coarse_all, 4: coarse_bottom})
    rows = restrict(lambda x: level_refs[1][6][x], blocks[1])

    gath_s[me["gx"], me["gy"], me["gz"]] = into_message(rows)
    begin(line(1, gath_s))
    width1 = blocks[1][2]
    for x in range(blocks[1][0]):
        out1[x] = level_refs[1][7][x][:, :width1]
    finish(line(1, gath_s))
    begin(plane(1, gath_s))
    all_sent()
    finish(plane(1, gath_s))
    place(gath_s, src2)

    def neighbour_sum(below, d, above, width):
        second = d.shape[0]
        lane = lanes_of(d.shape)
        near = below + above
        up = pltpu.roll(d, 1, 0)
        down = pltpu.roll(d, second - 1, 0)
        up = jnp.concatenate((jnp.where(edge_row == 0, 0.0, up[:8]), up[8:]), 0)
        down = jnp.concatenate(
            (down[: second - 8], jnp.where(edge_row == 7, 0.0, down[second - 8 :])), 0
        )
        near += up + down
        left = pltpu.roll(d, 1, 1)
        right = pltpu.roll(d, LANES - 1, 1)
        if width == LANES:
            near += jnp.where(lane == 0, 0.0, left) + jnp.where(lane == LANES - 1, 0.0, right)
            return near
        return jnp.where(lane < width, near + left + right, 0.0)

    total_x, total_z, total_y = whole2
    zero = jnp.zeros((total_z, LANES), jnp.float32)
    scale, firsts, seconds = cheb_tables(
        DEGREE + 1, smooth_low, smooth_top + 4.0 ** (LEVELS - 1) * absorb_top
    )
    for slot in range(2):
        dir2[slot, 0] = zero
        dir2[slot, total_x + 1] = zero
    chunk = max(1, min(total_x, 256 // total_z))

    @pl.loop(0, total_x // chunk)
    def _(n):
        fields = [src2[n * chunk + j] * scale for j in range(chunk)]
        for j in range(chunk):
            dir2[0, n * chunk + j + 1] = fields[j]
            it2[n * chunk + j] = fields[j]

    for r in range(DEGREE + 1):
        old, new = r % 2, (r + 1) % 2

        @pl.loop(0, total_x // chunk)
        def _(n, r=r, old=old, new=new):
            xs = [n * chunk + j for j in range(chunk)]
            layers = [dir2[old, xs[0] + j] for j in range(chunk + 2)]
            bases = [(src2 if r in (0, DEGREE) else res2)[x] for x in xs]
            parts = [coef2[x] for x in xs]
            results = []
            for j in range(chunk):
                near = neighbour_sum(layers[j], layers[j + 1], layers[j + 2], total_y)
                results.append(bases[j] - ((6.0 + parts[j]) * layers[j + 1] - near))
            if r < DEGREE:
                fields = [
                    firsts[r] * layers[j + 1] + seconds[r] * results[j] for j in range(chunk)
                ]
                totals = [it2[x] + d for x, d in zip(xs, fields)]
                for j, x in enumerate(xs):
                    it2[x] = totals[j]
                    dir2[new, x + 1] = totals[j] if r == DEGREE - 1 else fields[j]
            for j, x in enumerate(xs):
                res2[x] = results[j]

    spread(restrict(lambda x: res2[x], whole2), whole3, src3)

    whole_x, whole_z, whole_y = whole3
    zero = jnp.zeros((whole_z, LANES), jnp.float32)
    for ref in (dir3, it3):
        ref[0] = zero
        ref[whole_x + 1] = zero
    for x in range(whole_x):
        source = src3[x]
        res3[x] = source
        dir3[x + 1] = source * bottom_scale
        it3[x + 1] = source * bottom_scale

    def bottom_turn(n, carry):
        one = tab[0, n]
        two = tab[1, n]
        layers = [dir3[x] for x in range(whole_x + 2)]
        bases = [res3[x] for x in range(whole_x)]
        for x in range(whole_x):
            near = neighbour_sum(layers[x], layers[x + 1], layers[x + 2], whole_y)
            res = bases[x] - ((6.0 + coef3[x]) * layers[x + 1] - near)
            d = one * layers[x + 1] + two * res
            res3[x] = res
            dir3[x + 1] = d
            it3[x + 1] += d
        return carry

    lax.fori_loop(0, BOTTOM_ITERS - 1, bottom_turn, 0)

    i = lanes_of((LANES, LANES))
    along_y = jnp.where(
        i < width2, trilinear(rows_of((LANES, LANES)), me["gy"] * width2 + i), 0.0
    )
    along_z = trilinear(
        lanes_of((second2, whole_z)), me["gz"] * second2 + rows_of((second2, whole_z))
    )
    layers = []
    for x in range(first2):
        centre = me["gx"] * (first2 // 2) + x // 2 + 1
        layers.append(0.75 * it3[centre] + 0.25 * it3[centre + 2 * (x % 2) - 1])
    moved = exact_dot(jnp.concatenate(layers, axis=0), along_y)
    own_rows = pl.ds(pl.multiple_of(me["gz"] * second2, second2), second2)
    back = lax.rem(LANES - me["gy"] * width2, LANES)
    for x in range(first2):
        fine = exact_dot(along_z, moved[x * whole_z : (x + 1) * whole_z])
        own = pltpu.roll(it2[me["gx"] * first2 + x, own_rows, :], back, 1)
        out2[x] = (own + fine)[:, :width2]


def on_device(sizes, right_side, absorption):
    nx, nz, ny = sizes
    blocks = [tuple(s // 2**k for s in right_side.shape) for k in range(LEVELS)]
    rounds = DEGREE + 1
    scratch = []
    for first, second, width in blocks[:SPLIT]:
        scratch += [
            pltpu.VMEM((rounds, first + 2, second, LANES), jnp.float32),
            pltpu.VMEM((rounds, 2, first, LANES), jnp.float32),
            pltpu.VMEM((rounds, second, LANES), jnp.float32),
            pltpu.VMEM((rounds, 2, second, LANES), jnp.float32),
            pltpu.VMEM((rounds, 2, first, LANES), jnp.float32),
            pltpu.VMEM((rounds, 2, second, LANES), jnp.float32),
            pltpu.VMEM((first, second, LANES), jnp.float32),
            pltpu.VMEM((first, second, LANES), jnp.float32),
            pltpu.VMEM((2, first, second, LANES), jnp.float32),
        ]
    first2, second2, _ = blocks[2]
    x2, z2 = first2 * nx, second2 * nz
    x3, z3 = x2 // 2, z2 // 2
    pair_rows = max(blocks[0][0] // 2 * blocks[0][1], x2 // 2 * z2)
    lines = nz - 1 + nx * ny - 1
    scratch += [
        pltpu.VMEM(right_side.shape, jnp.float32),
        pltpu.VMEM(right_side.shape, jnp.float32),
        pltpu.VMEM((pair_rows, LANES), jnp.float32),
        pltpu.VMEM((nx, ny, nz, second2, LANES), jnp.float32),
        pltpu.VMEM((nx, ny, nz, second2, LANES), jnp.float32),
        pltpu.VMEM((x2, z2, LANES), jnp.float32),
        pltpu.VMEM((x2, z2, LANES), jnp.float32),
        pltpu.VMEM((2, x2 + 2, z2, LANES), jnp.float32),
        pltpu.VMEM((x2, z2, LANES), jnp.float32),
        pltpu.VMEM((x2, z2, LANES), jnp.float32),
        pltpu.VMEM((x3, z3, LANES), jnp.float32),
        pltpu.VMEM((x3, z3, LANES), jnp.float32),
        pltpu.VMEM((x3 + 2, z3, LANES), jnp.float32),
        pltpu.VMEM((x3, z3, LANES), jnp.float32),
        pltpu.VMEM((x3 + 2, z3, LANES), jnp.float32),
        pltpu.SMEM((2, BOTTOM_ITERS - 1), jnp.float32),
        pltpu.SemaphoreType.DMA((SPLIT * rounds, 6)),
        pltpu.SemaphoreType.DMA((SPLIT * rounds, 6)),
        pltpu.SemaphoreType.DMA((2, lines)),
        pltpu.SemaphoreType.DMA((2, lines)),
        pltpu.SemaphoreType.DMA((2,)),
    ]
    vmem = pl.BlockSpec(memory_space=pltpu.VMEM)
    return pl.pallas_call(
        functools.partial(kernel, sizes, blocks),
        out_shape=tuple(jax.ShapeDtypeStruct(b, jnp.float32) for b in blocks),
        in_specs=[pl.BlockSpec(memory_space=pltpu.HBM)] * 2,
        out_specs=(vmem, vmem, vmem),
        scratch_shapes=scratch,
        compiler_params=pltpu.CompilerParams(
            collective_id=0, has_side_effects=True, vmem_limit_bytes=63 * 1024 * 1024
        ),
    )(right_side, absorption)


def solution(mesh):
    sizes = tuple(mesh.shape[a] for a in AXES)
    spec = P("gx", "gz", "gy")
    return jax.shard_map(
        functools.partial(on_device, sizes),
        mesh=mesh,
        in_specs=(spec, spec),
        out_specs=(spec, spec, spec),
        check_vma=False,
    )
```

```python
import functools

import jax
import jax.numpy as jnp
from jax import lax
from jax.experimental import pallas as pl
from jax.experimental.pallas import tpu as pltpu
from jax.sharding import PartitionSpec as P

DEGREE = 4
LEVELS = 3
SPLIT = 2
BOTTOM_ITERS = 20
LANES = 128

smooth_low = 1.5
smooth_top = 12.0
absorb_top = 1.0
bottom_low = 0.008

MESH = pl.DeviceIdType.MESH
AXES = ("gx", "gz", "gy")


def cheb_tables(count, lower, upper):
    theta = (upper + lower) / 2.0
    delta = (upper - lower) / 2.0
    sigma = theta / delta
    rho_value = 1.0 / sigma
    firsts = []
    seconds = []
    for turn_index in range(count - 1):
        rho_next = 1.0 / (2.0 * sigma - rho_value)
        firsts.append(rho_next * rho_value)
        seconds.append(2.0 * rho_next / delta)
        rho_value = rho_next
    return (1.0 / theta, firsts, seconds)


def exact_dot(left, right):
    return jnp.dot(
        left, right, precision=lax.Precision.HIGHEST, preferred_element_type=jnp.float32
    )


def lanes_of(shape):
    return lax.broadcasted_iota(jnp.int32, shape, len(shape) - 1)


def rows_of(shape):
    return lax.broadcasted_iota(jnp.int32, shape, len(shape) - 2)


def halving():
    j = rows_of((LANES, LANES))
    i = lanes_of((LANES, LANES))
    return jnp.where(j // 2 == i, jnp.float32(0.5), jnp.float32(0.0))


def trilinear(coarse, fine):
    centre = fine // 2
    other = centre + 2 * (fine % 2) - 1
    return jnp.where(coarse == centre, jnp.float32(0.75), jnp.float32(0.0)) + jnp.where(
        coarse == other, jnp.float32(0.25), jnp.float32(0.0)
    )


def kernel(sizes, blocks, rs_hbm, ab_hbm, out0, out1, out2, *scratch):
    nx, nz, ny = sizes
    me = {a: lax.axis_index(a) for a in AXES}
    count = dict(zip(AXES, sizes))
    has_lo = {a: me[a] > 0 for a in AXES}
    has_hi = {a: me[a] < count[a] - 1 for a in AXES}

    per_level = 9
    level_refs = [list(scratch[per_level * k : per_level * (k + 1)]) for k in range(SPLIT)]
    level_refs[0][7] = out0
    rest = scratch[per_level * SPLIT :]
    rs, ab, pairs, gath_s, gath_c, src2, coef2, dir2, res2, it2 = rest[:10]
    src3, coef3, dir3, res3, it3, tab = rest[10:16]
    send_sem, recv_sem, gsend, grecv, fetch_sem = rest[16:]

    fetches = [
        pltpu.make_async_copy(rs_hbm, rs, fetch_sem.at[0]),
        pltpu.make_async_copy(ab_hbm, ab, fetch_sem.at[1]),
    ]
    for fetch in fetches:
        fetch.start()

    scales = []
    for level in range(LEVELS + 1):
        turns, lower = (BOTTOM_ITERS, bottom_low) if level == LEVELS else (DEGREE + 1, smooth_low)
        scale, firsts, seconds = cheb_tables(turns, lower, smooth_top + 4.0**level * absorb_top)
        scales.append(scale)
        for n in range(turns - 1):
            tab[2 * level, n] = jnp.float32(firsts[n])
            tab[2 * level + 1, n] = jnp.float32(seconds[n])
    bottom_scale = scales[LEVELS]

    z_peers = [{"gz": k} for k in range(1, nz)]
    plane_peers = [
        {"gx": i, "gy": j} for i in range(nx) for j in range(ny) if (i, j) != (0, 0)
    ]

    def device(offsets):
        return {a: lax.rem(me[a] + k, count[a]) for a, k in offsets.items()}

    barrier = pltpu.get_barrier_semaphore()
    for peer in z_peers + plane_peers:
        pl.semaphore_signal(barrier, inc=1, device_id=device(peer), device_id_type=MESH)

    half = halving()

    def restrict(read, shape):
        first, second, _ = shape
        for x in range(first // 2):
            pairs[pl.ds(x * second, second), :] = read(2 * x) + read(2 * x + 1)
        total = first // 2 * second // 2
        summed = (
            pairs[pl.ds(0, total, stride=2), :] + pairs[pl.ds(1, total, stride=2), :]
        )
        return exact_dot(summed, half)

    def copies(level, r):
        first, second, _ = blocks[level]
        dirs, faces_z, faces_y, halo_x, halo_z, halo_y = level_refs[level][:6]
        slot = level * (DEGREE + 1) + r
        ends = {
            "gx": (dirs.at[r, 1], dirs.at[r, first], halo_x),
            "gz": (faces_z.at[r, 0], faces_z.at[r, 1], halo_z),
            "gy": (faces_y.at[r], faces_y.at[r], halo_y),
        }
        made = []
        for n, a in enumerate(AXES):
            low_face, high_face, halo = ends[a]
            made.append(
                (
                    has_lo[a],
                    has_hi[a],
                    pltpu.make_async_remote_copy(
                        src_ref=low_face,
                        dst_ref=halo.at[r, 1],
                        send_sem=send_sem.at[slot, 2 * n],
                        recv_sem=recv_sem.at[slot, 2 * n],
                        device_id={a: jnp.maximum(me[a] - 1, 0)},
                        device_id_type=MESH,
                    ),
                )
            )
            made.append(
                (
                    has_hi[a],
                    has_lo[a],
                    pltpu.make_async_remote_copy(
                        src_ref=high_face,
                        dst_ref=halo.at[r, 0],
                        send_sem=send_sem.at[slot, 2 * n + 1],
                        recv_sem=recv_sem.at[slot, 2 * n + 1],
                        device_id={a: jnp.minimum(me[a] + 1, count[a] - 1)},
                        device_id_type=MESH,
                    ),
                )
            )
        return made

    def start(level, r, part):
        for sends, _, copy in copies(level, r)[part]:
            pl.when(sends)(copy.start)

    along_x, along_zy = slice(0, 2), slice(2, 6)

    def arrive(level, r):
        for _, gets, copy in copies(level, r):
            pl.when(gets)(copy.wait_recv)

    def all_sent():
        rounds = [copies(level, r) for level in range(SPLIT) for r in range(DEGREE + 1)]
        for way in range(6):

            @pl.when(rounds[0][way][0])
            def _(way=way):
                for made in rounds:
                    made[way][2].wait_send()

    def put_faces(level, r, x, field, packed):
        second, width = blocks[level][1:]
        dirs, faces_z = level_refs[level][:2]
        dirs[r, x + 1] = field
        faces_z[r, 0, pl.ds(x, 1), :] = field[:1]
        faces_z[r, 1, pl.ds(x, 1), :] = field[second - 1 :]
        lane = lanes_of((second, LANES))
        low = pltpu.roll(field, 2 * x + 1, 1)
        if width == LANES:
            return jnp.where(lane // 2 == x, low, packed)
        high = pltpu.roll(field, 2 * x + LANES + 1 - width, 1)
        return jnp.where(lane == 2 * x + 1, low, jnp.where(lane == 2 * x, high, packed))

    def by_chunks(level, body, carry, ends_done=None):
        first, second, _ = blocks[level]
        chunk = min(first, 256 // second)
        turns = first // chunk

        def turn(n, carry):
            if turns > 2:
                chosen = jnp.where(n == 0, 0, jnp.where(n == 1, turns - 1, n - 1))
            else:
                chosen = n
            carry = body([chosen * chunk + j for j in range(chunk)], carry)
            if ends_done is not None and turns > 1:
                pl.when(n == 1)(ends_done)
            return carry

        if turns == 1:
            carry = turn(0, carry)
            if ends_done is not None:
                ends_done()
            return carry
        return lax.fori_loop(0, turns, turn, carry)

    edge_row = rows_of((8, LANES))

    def inside(level, r, base, coef):
        first, second, width = blocks[level]
        dirs = level_refs[level][0]
        resid = level_refs[level][6]
        lane = lanes_of((second, LANES))

        def body(xs, carry):
            layers = [dirs[r, xs[0] + j] for j in range(len(xs) + 2)]
            bases = [base[x] for x in xs]
            parts = [coef[x] for x in xs]
            results = []
            for j in range(len(xs)):
                d = layers[j + 1]
                near = layers[j] + layers[j + 2]
                up = pltpu.roll(d, 1, 0)
                down = pltpu.roll(d, second - 1, 0)
                up = jnp.concatenate((jnp.where(edge_row == 0, 0.0, up[:8]), up[8:]), 0)
                down = jnp.concatenate(
                    (down[: second - 8], jnp.where(edge_row == 7, 0.0, down[second - 8 :])), 0
                )
                near += up + down
                near += pltpu.roll(d, 1, 1) + pltpu.roll(d, LANES - 1, 1)
                if width < LANES:
                    near = jnp.where(lane < width, near, 0.0)
                results.append(bases[j] - ((6.0 + parts[j]) * d - near))
            for j, x in enumerate(xs):
                resid[x] = results[j]
            return carry

        by_chunks(level, body, 0)

    def outside(level, r):
        first, second, width = blocks[level]
        faces_y, halo_x, halo_z, halo_y = level_refs[level][2:6]
        resid = level_refs[level][6]
        lane = lanes_of((second, LANES))
        resid[0] += jnp.where(has_lo["gx"], halo_x[r, 0], 0.0)
        resid[first - 1] += jnp.where(has_hi["gx"], halo_x[r, 1], 0.0)
        low = jnp.where(has_lo["gy"], halo_y[r, 0], 0.0)
        high = jnp.where(has_hi["gy"], halo_y[r, 1], 0.0)
        if width == LANES:
            low -= faces_y[r]
            high -= faces_y[r]
        ends = jnp.where(lane % 2 == 1, pltpu.roll(low, 1, 1), pltpu.roll(high, LANES - 1, 1))

        def add(x):
            res = resid[x]
            z_low = jnp.where(has_lo["gz"], halo_z[r, 0, pl.ds(x, 1), :], 0.0)
            z_high = jnp.where(has_hi["gz"], halo_z[r, 1, pl.ds(x, 1), :], 0.0)
            res = jnp.concatenate(
                (
                    res[:8] + jnp.where(edge_row == 0, z_low, 0.0),
                    res[8 : second - 8],
                    res[second - 8 :] + jnp.where(edge_row == 7, z_high, 0.0),
                )[:: 1 if second > 16 else 2],
                0,
            )
            to_low = pltpu.roll(ends, LANES - 1 - 2 * x, 1)
            if width == LANES:
                res += jnp.where((lane == 0) | (lane == LANES - 1), to_low, 0.0)
            else:
                to_high = pltpu.roll(ends, width - 1 - 2 * x, 1)
                res += jnp.where(lane == 0, to_low, jnp.where(lane == width - 1, to_high, 0.0))
            return res

        return add

    def smooth(level, source, coef, between, last_work=None):
        first, second, width = blocks[level]
        dirs, _, faces_y = level_refs[level][:3]
        resid, iterate = level_refs[level][6:8]
        scale = scales[level]
        empty = jnp.zeros((second, LANES), jnp.float32)
        for r in range(DEGREE + 1):
            dirs[r, 0] = empty
            dirs[r, first + 1] = empty

        def opening(xs, packed):
            fields = [source[x] * scale for x in xs]
            for x, d in zip(xs, fields):
                iterate[x] = d
                resid[x] = source[x]
                packed = put_faces(level, 0, x, d, packed)
            return packed

        faces_y[0] = by_chunks(level, opening, empty)
        if level == 0:
            pl.semaphore_wait(barrier, len(z_peers) + len(plane_peers))
        start(level, 0, along_x)
        if level == 0:
            fetches[1].wait()

        @pl.loop(0, DEGREE)
        def _(r):
            one = tab[2 * level, r]
            two = tab[2 * level + 1, r]
            start(level, r, along_zy)
            inside(level, r, resid, coef)
            for when, work in between.items():
                pl.when(r == when)(work)
            arrive(level, r)
            add = outside(level, r)

            def turn(xs, packed):
                results = [add(x) for x in xs]
                fields = [one * dirs[r, x + 1] + two * res for x, res in zip(xs, results)]
                totals = [iterate[x] + d for x, d in zip(xs, fields)]
                for x, res, d, total in zip(xs, results, fields, totals):
                    resid[x] = res
                    iterate[x] = total
                    sent = jnp.where(r == DEGREE - 1, total, d)
                    packed = put_faces(level, r + 1, x, sent, packed)
                return packed

            faces_y[r + 1] = by_chunks(
                level, turn, empty, lambda: start(level, r + 1, along_x)
            )

        start(level, DEGREE, along_zy)
        inside(level, DEGREE, source, coef)
        if last_work is not None:
            last_work()
        arrive(level, DEGREE)
        add = outside(level, DEGREE)

        def last(xs, carry):
            results = [add(x) for x in xs]
            for x, res in zip(xs, results):
                resid[x] = res
            return carry

        by_chunks(level, last, 0)

    coef1, source1 = level_refs[1][8].at[0], level_refs[1][8].at[1]
    first2, second2, width2 = blocks[2]
    whole2 = (first2 * nx, second2 * nz, width2 * ny)
    whole3 = tuple(s // 2 for s in whole2)

    def spread(rows, shape, ref):
        for x in range(shape[0]):
            ref[x] = rows[x * shape[1] : (x + 1) * shape[1]]

    def into_message(rows):
        packed = rows[:second2]
        for x in range(1, first2):
            packed += pltpu.roll(rows[x * second2 : (x + 1) * second2], x * width2, 1)
        return packed

    def line(which, gath):
        piece = gath.at[me["gx"], me["gy"], me["gz"]]
        return gather(piece, which, z_peers, 0)

    def plane(which, gath):
        piece = gath.at[me["gx"], me["gy"]]
        return gather(piece, which, plane_peers, len(z_peers))

    def gather(piece, which, peers, base):
        return [
            pltpu.make_async_remote_copy(
                src_ref=piece,
                dst_ref=piece,
                send_sem=gsend.at[which, base + k],
                recv_sem=grecv.at[which, base + k],
                device_id=device(peer),
                device_id_type=MESH,
            )
            for k, peer in enumerate(peers)
        ]

    def begin(copies):
        for copy in copies:
            copy.start()

    def finish(copies):
        for copy in copies:
            copy.wait_recv()
        for copy in copies:
            copy.wait_send()

    def place(gath, ref):
        lane = lanes_of((second2, LANES))

        @pl.loop(0, nx * nz // 2)
        def _(n):
            for m in (2 * n, 2 * n + 1):
                ix = m // nz
                iz = m % nz
                held = [gath[ix, iy, iz] for iy in range(ny)]
                for x in range(first2):
                    tile = jnp.zeros((second2, LANES), jnp.float32)
                    for iy in range(ny):
                        shift = (iy - x) * width2 % LANES
                        moved = pltpu.roll(held[iy], shift, 1) if shift else held[iy]
                        tile = jnp.where(lane // width2 == iy, moved, tile)
                    start_row = pl.multiple_of(iz * second2, second2)
                    ref[ix * first2 + x, pl.ds(start_row, second2), :] = tile

    def coarsen():
        spread(restrict(lambda x: ab[x], blocks[0]), blocks[1], coef1)
        rows = restrict(lambda x: coef1[x], blocks[1])
        gath_c[me["gx"], me["gy"], me["gz"]] = into_message(rows)
        begin(line(0, gath_c))

    def coarse_plane():
        finish(line(0, gath_c))
        begin(plane(0, gath_c))

    def coarse_all():
        finish(plane(0, gath_c))
        place(gath_c, coef2)

    def coarse_bottom():
        spread(restrict(lambda x: coef2[x], whole2), whole3, coef3)

    fetches[0].wait()
    smooth(0, rs, ab, {0: coarsen})
    resid = level_refs[0][6]
    spread(restrict(lambda x: resid[x], blocks[0]), blocks[1], source1)
    smooth(1, source1, coef1, {0: coarse_plane, 3: coarse_all}, coarse_bottom)
    rows = restrict(lambda x: level_refs[1][6][x], blocks[1])

    gath_s[me["gx"], me["gy"], me["gz"]] = into_message(rows)
    begin(line(1, gath_s))
    width1 = blocks[1][2]
    for x in range(blocks[1][0]):
        out1[x] = level_refs[1][7][x][:, :width1]
    finish(line(1, gath_s))
    begin(plane(1, gath_s))
    all_sent()
    finish(plane(1, gath_s))
    place(gath_s, src2)

    def neighbour_sum(below, d, above, width):
        second = d.shape[0]
        lane = lanes_of(d.shape)
        near = below + above
        up = pltpu.roll(d, 1, 0)
        down = pltpu.roll(d, second - 1, 0)
        up = jnp.concatenate((jnp.where(edge_row == 0, 0.0, up[:8]), up[8:]), 0)
        down = jnp.concatenate(
            (down[: second - 8], jnp.where(edge_row == 7, 0.0, down[second - 8 :])), 0
        )
        near += up + down
        left = pltpu.roll(d, 1, 1)
        right = pltpu.roll(d, LANES - 1, 1)
        if width == LANES:
            near += jnp.where(lane == 0, 0.0, left) + jnp.where(lane == LANES - 1, 0.0, right)
            return near
        return jnp.where(lane < width, near + left + right, 0.0)

    total_x, total_z, total_y = whole2
    zero = jnp.zeros((total_z, LANES), jnp.float32)
    scale = scales[LEVELS - 1]
    for slot in range(2):
        dir2[slot, 0] = zero
        dir2[slot, total_x + 1] = zero
    chunk = max(1, min(total_x, 256 // total_z))

    @pl.loop(0, total_x // chunk)
    def _(n):
        fields = [src2[n * chunk + j] * scale for j in range(chunk)]
        for j in range(chunk):
            dir2[0, n * chunk + j + 1] = fields[j]
            it2[n * chunk + j] = fields[j]
            res2[n * chunk + j] = src2[n * chunk + j]

    def whole_turn(r, base, store):
        old = lax.rem(r, 2)

        @pl.loop(0, total_x // chunk)
        def _(n):
            xs = [n * chunk + j for j in range(chunk)]
            layers = [dir2[old, xs[0] + j] for j in range(chunk + 2)]
            bases = [base[x] for x in xs]
            parts = [coef2[x] for x in xs]
            results = []
            for j in range(chunk):
                near = neighbour_sum(layers[j], layers[j + 1], layers[j + 2], total_y)
                results.append(bases[j] - ((6.0 + parts[j]) * layers[j + 1] - near))
            store(xs, layers, results)
            for j, x in enumerate(xs):
                res2[x] = results[j]

    @pl.loop(0, DEGREE)
    def _(r):
        one = tab[2 * LEVELS - 2, r]
        two = tab[2 * LEVELS - 1, r]
        new = lax.rem(r + 1, 2)

        def store(xs, layers, results):
            fields = [one * layers[j + 1] + two * results[j] for j in range(chunk)]
            totals = [it2[x] + d for x, d in zip(xs, fields)]
            for j, x in enumerate(xs):
                it2[x] = totals[j]
                dir2[new, x + 1] = jnp.where(r == DEGREE - 1, totals[j], fields[j])

        whole_turn(r, res2, store)

    whole_turn(jnp.int32(DEGREE), src2, lambda xs, layers, results: None)

    spread(restrict(lambda x: res2[x], whole2), whole3, src3)

    whole_x, whole_z, whole_y = whole3
    zero = jnp.zeros((whole_z, LANES), jnp.float32)
    for ref in (dir3, it3):
        ref[0] = zero
        ref[whole_x + 1] = zero
    for x in range(whole_x):
        source = src3[x]
        res3[x] = source
        dir3[x + 1] = source * bottom_scale
        it3[x + 1] = source * bottom_scale

    def bottom_turn(n, carry):
        one = tab[2 * LEVELS, n]
        two = tab[2 * LEVELS + 1, n]
        layers = [dir3[x] for x in range(whole_x + 2)]
        bases = [res3[x] for x in range(whole_x)]
        for x in range(whole_x):
            near = neighbour_sum(layers[x], layers[x + 1], layers[x + 2], whole_y)
            res = bases[x] - ((6.0 + coef3[x]) * layers[x + 1] - near)
            d = one * layers[x + 1] + two * res
            res3[x] = res
            dir3[x + 1] = d
            it3[x + 1] += d
        return carry

    lax.fori_loop(0, BOTTOM_ITERS - 1, bottom_turn, 0)

    i = lanes_of((LANES, LANES))
    along_y = jnp.where(
        i < width2, trilinear(rows_of((LANES, LANES)), me["gy"] * width2 + i), 0.0
    )
    along_z = trilinear(
        lanes_of((second2, whole_z)), me["gz"] * second2 + rows_of((second2, whole_z))
    )
    layers = []
    for x in range(first2):
        centre = me["gx"] * (first2 // 2) + x // 2 + 1
        layers.append(0.75 * it3[centre] + 0.25 * it3[centre + 2 * (x % 2) - 1])
    moved = exact_dot(jnp.concatenate(layers, axis=0), along_y)
    own_rows = pl.ds(pl.multiple_of(me["gz"] * second2, second2), second2)
    back = lax.rem(LANES - me["gy"] * width2, LANES)
    for x in range(first2):
        fine = exact_dot(along_z, moved[x * whole_z : (x + 1) * whole_z])
        own = pltpu.roll(it2[me["gx"] * first2 + x, own_rows, :], back, 1)
        out2[x] = (own + fine)[:, :width2]


def on_device(sizes, right_side, absorption):
    nx, nz, ny = sizes
    blocks = [tuple(s // 2**k for s in right_side.shape) for k in range(LEVELS)]
    rounds = DEGREE + 1
    scratch = []
    for first, second, width in blocks[:SPLIT]:
        scratch += [
            pltpu.VMEM((rounds, first + 2, second, LANES), jnp.float32),
            pltpu.VMEM((rounds, 2, first, LANES), jnp.float32),
            pltpu.VMEM((rounds, second, LANES), jnp.float32),
            pltpu.VMEM((rounds, 2, second, LANES), jnp.float32),
            pltpu.VMEM((rounds, 2, first, LANES), jnp.float32),
            pltpu.VMEM((rounds, 2, second, LANES), jnp.float32),
            pltpu.VMEM((first, second, LANES), jnp.float32),
            pltpu.VMEM((first, second, LANES), jnp.float32),
            pltpu.VMEM((2, first, second, LANES), jnp.float32),
        ]
    first2, second2, _ = blocks[2]
    x2, z2 = first2 * nx, second2 * nz
    x3, z3 = x2 // 2, z2 // 2
    pair_rows = max(blocks[0][0] // 2 * blocks[0][1], x2 // 2 * z2)
    lines = nz - 1 + nx * ny - 1
    scratch += [
        pltpu.VMEM(right_side.shape, jnp.float32),
        pltpu.VMEM(right_side.shape, jnp.float32),
        pltpu.VMEM((pair_rows, LANES), jnp.float32),
        pltpu.VMEM((nx, ny, nz, second2, LANES), jnp.float32),
        pltpu.VMEM((nx, ny, nz, second2, LANES), jnp.float32),
        pltpu.VMEM((x2, z2, LANES), jnp.float32),
        pltpu.VMEM((x2, z2, LANES), jnp.float32),
        pltpu.VMEM((2, x2 + 2, z2, LANES), jnp.float32),
        pltpu.VMEM((x2, z2, LANES), jnp.float32),
        pltpu.VMEM((x2, z2, LANES), jnp.float32),
        pltpu.VMEM((x3, z3, LANES), jnp.float32),
        pltpu.VMEM((x3, z3, LANES), jnp.float32),
        pltpu.VMEM((x3 + 2, z3, LANES), jnp.float32),
        pltpu.VMEM((x3, z3, LANES), jnp.float32),
        pltpu.VMEM((x3 + 2, z3, LANES), jnp.float32),
        pltpu.SMEM((2 * LEVELS + 2, BOTTOM_ITERS - 1), jnp.float32),
        pltpu.SemaphoreType.DMA((SPLIT * rounds, 6)),
        pltpu.SemaphoreType.DMA((SPLIT * rounds, 6)),
        pltpu.SemaphoreType.DMA((2, lines)),
        pltpu.SemaphoreType.DMA((2, lines)),
        pltpu.SemaphoreType.DMA((2,)),
    ]
    vmem = pl.BlockSpec(memory_space=pltpu.VMEM)
    return pl.pallas_call(
        functools.partial(kernel, sizes, blocks),
        out_shape=tuple(jax.ShapeDtypeStruct(b, jnp.float32) for b in blocks),
        in_specs=[pl.BlockSpec(memory_space=pltpu.HBM)] * 2,
        out_specs=(vmem, vmem, vmem),
        scratch_shapes=scratch,
        compiler_params=pltpu.CompilerParams(
            collective_id=0, has_side_effects=True, vmem_limit_bytes=63 * 1024 * 1024
        ),
    )(right_side, absorption)


def solution(mesh):
    sizes = tuple(mesh.shape[a] for a in AXES)
    spec = P("gx", "gz", "gy")
    return jax.shard_map(
        functools.partial(on_device, sizes),
        mesh=mesh,
        in_specs=(spec, spec),
        out_specs=(spec, spec, spec),
        check_vma=False,
    )
```

```python
import functools

import jax
import jax.numpy as jnp
from jax import lax
from jax.experimental import pallas as pl
from jax.experimental.pallas import tpu as pltpu
from jax.sharding import PartitionSpec as P

DEGREE = 4
LEVELS = 3
SPLIT = 2
BOTTOM_ITERS = 20
LANES = 128

smooth_low = 1.5
smooth_top = 12.0
absorb_top = 1.0
bottom_low = 0.008

MESH = pl.DeviceIdType.MESH
AXES = ("gx", "gz", "gy")


def cheb_tables(count, lower, upper):
    theta = (upper + lower) / 2.0
    delta = (upper - lower) / 2.0
    sigma = theta / delta
    rho_value = 1.0 / sigma
    firsts = []
    seconds = []
    for turn_index in range(count - 1):
        rho_next = 1.0 / (2.0 * sigma - rho_value)
        firsts.append(rho_next * rho_value)
        seconds.append(2.0 * rho_next / delta)
        rho_value = rho_next
    return (1.0 / theta, firsts, seconds)


def exact_dot(left, right):
    return jnp.dot(
        left, right, precision=lax.Precision.HIGHEST, preferred_element_type=jnp.float32
    )


def lanes_of(shape):
    return lax.broadcasted_iota(jnp.int32, shape, len(shape) - 1)


def rows_of(shape):
    return lax.broadcasted_iota(jnp.int32, shape, len(shape) - 2)


def halving():
    j = rows_of((LANES, LANES))
    i = lanes_of((LANES, LANES))
    return jnp.where(j // 2 == i, jnp.float32(0.5), jnp.float32(0.0))


def trilinear(coarse, fine):
    centre = fine // 2
    other = centre + 2 * (fine % 2) - 1
    return jnp.where(coarse == centre, jnp.float32(0.75), jnp.float32(0.0)) + jnp.where(
        coarse == other, jnp.float32(0.25), jnp.float32(0.0)
    )


def kernel(sizes, blocks, rs_hbm, ab_hbm, out0, out1, out2, *scratch):
    nx, nz, ny = sizes
    me = {a: lax.axis_index(a) for a in AXES}
    count = dict(zip(AXES, sizes))
    has_lo = {a: me[a] > 0 for a in AXES}
    has_hi = {a: me[a] < count[a] - 1 for a in AXES}

    per_level = 9
    level_refs = [list(scratch[per_level * k : per_level * (k + 1)]) for k in range(SPLIT)]
    rest = scratch[per_level * SPLIT :]
    rs, ab, pairs, gath_s, gath_c, src2, coef2, dir2, res2, it2 = rest[:10]
    src3, coef3, dir3, res3, it3, tab = rest[10:16]
    send_sem, recv_sem, gsend, grecv, fetch_sem, narrow = rest[16:]

    fetches = [
        pltpu.make_async_copy(rs_hbm, rs, fetch_sem.at[0]),
        pltpu.make_async_copy(ab_hbm, ab, fetch_sem.at[1]),
    ]
    for fetch in fetches:
        fetch.start()

    bottom_scale, firsts, seconds = cheb_tables(
        BOTTOM_ITERS, bottom_low, smooth_top + 4.0**LEVELS * absorb_top
    )
    for n in range(BOTTOM_ITERS - 1):
        tab[0, n] = jnp.float32(firsts[n])
        tab[1, n] = jnp.float32(seconds[n])

    z_peers = [{"gz": k} for k in range(1, nz)]
    plane_peers = [
        {"gx": i, "gy": j} for i in range(nx) for j in range(ny) if (i, j) != (0, 0)
    ]

    def device(offsets):
        return {a: lax.rem(me[a] + k, count[a]) for a, k in offsets.items()}

    barrier = pltpu.get_barrier_semaphore()
    for peer in z_peers + plane_peers:
        pl.semaphore_signal(barrier, inc=1, device_id=device(peer), device_id_type=MESH)

    half = halving()

    def restrict(read, shape):
        first, second, _ = shape
        for x in range(first // 2):
            pairs[pl.ds(x * second, second), :] = read(2 * x) + read(2 * x + 1)
        total = first // 2 * second // 2
        summed = (
            pairs[pl.ds(0, total, stride=2), :] + pairs[pl.ds(1, total, stride=2), :]
        )
        return exact_dot(summed, half)

    def copies(level, r):
        first, second, _ = blocks[level]
        dirs, faces_z, faces_y, halo_x, halo_z, halo_y = level_refs[level][:6]
        slot = level * (DEGREE + 1) + r
        ends = {
            "gx": (dirs.at[r, 1], dirs.at[r, first], halo_x),
            "gz": (faces_z.at[r, 0], faces_z.at[r, 1], halo_z),
            "gy": (faces_y.at[r], faces_y.at[r], halo_y),
        }
        made = []
        for n, a in enumerate(AXES):
            low_face, high_face, halo = ends[a]
            made.append(
                (
                    has_lo[a],
                    has_hi[a],
                    pltpu.make_async_remote_copy(
                        src_ref=low_face,
                        dst_ref=halo.at[r, 1],
                        send_sem=send_sem.at[slot, 2 * n],
                        recv_sem=recv_sem.at[slot, 2 * n],
                        device_id={a: jnp.maximum(me[a] - 1, 0)},
                        device_id_type=MESH,
                    ),
                )
            )
            made.append(
                (
                    has_hi[a],
                    has_lo[a],
                    pltpu.make_async_remote_copy(
                        src_ref=high_face,
                        dst_ref=halo.at[r, 0],
                        send_sem=send_sem.at[slot, 2 * n + 1],
                        recv_sem=recv_sem.at[slot, 2 * n + 1],
                        device_id={a: jnp.minimum(me[a] + 1, count[a] - 1)},
                        device_id_type=MESH,
                    ),
                )
            )
        return made

    def start(level, r, part):
        for sends, _, copy in copies(level, r)[part]:
            pl.when(sends)(copy.start)

    along_x, along_zy = slice(0, 2), slice(2, 6)

    def arrive(level, r):
        for _, gets, copy in copies(level, r):
            pl.when(gets)(copy.wait_recv)

    def all_sent():
        rounds = [copies(level, r) for level in range(SPLIT) for r in range(DEGREE + 1)]
        for way in range(6):

            @pl.when(rounds[0][way][0])
            def _(way=way):
                for made in rounds:
                    made[way][2].wait_send()

    def put_faces(level, r, x, field, packed):
        second, width = blocks[level][1:]
        dirs, faces_z = level_refs[level][:2]
        dirs[r, x + 1] = field
        faces_z[r, 0, pl.ds(x, 1), :] = field[:1]
        faces_z[r, 1, pl.ds(x, 1), :] = field[second - 1 :]
        lane = lanes_of((second, LANES))
        low = pltpu.roll(field, 2 * x + 1, 1)
        if width == LANES:
            return jnp.where(lane // 2 == x, low, packed)
        high = pltpu.roll(field, 2 * x + LANES + 1 - width, 1)
        return jnp.where(lane == 2 * x + 1, low, jnp.where(lane == 2 * x, high, packed))

    def by_chunks(level, body, carry, ends_done=None, rows=256):
        first, second, _ = blocks[level]
        chunk = min(first, rows // second)
        turns = first // chunk

        def turn(n, carry):
            if turns > 2:
                chosen = jnp.where(n == 0, 0, jnp.where(n == 1, turns - 1, n - 1))
            else:
                chosen = n
            carry = body([chosen * chunk + j for j in range(chunk)], carry)
            if ends_done is not None and turns > 1:
                pl.when(n == 1)(ends_done)
            return carry

        if turns == 1:
            carry = turn(0, carry)
            if ends_done is not None:
                ends_done()
            return carry
        return lax.fori_loop(0, turns, turn, carry)

    edge_row = rows_of((8, LANES))

    def inside(level, r, base, coef):
        first, second, width = blocks[level]
        dirs = level_refs[level][0]
        resid = level_refs[level][6]
        lane = lanes_of((second, LANES))

        def body(xs, carry):
            layers = [dirs[r, xs[0] + j] for j in range(len(xs) + 2)]
            bases = [base[x] for x in xs]
            parts = [coef[x] for x in xs]
            results = []
            for j in range(len(xs)):
                d = layers[j + 1]
                near = layers[j] + layers[j + 2]
                up = pltpu.roll(d, 1, 0)
                down = pltpu.roll(d, second - 1, 0)
                up = jnp.concatenate((jnp.where(edge_row == 0, 0.0, up[:8]), up[8:]), 0)
                down = jnp.concatenate(
                    (down[: second - 8], jnp.where(edge_row == 7, 0.0, down[second - 8 :])), 0
                )
                near += up + down
                near += pltpu.roll(d, 1, 1) + pltpu.roll(d, LANES - 1, 1)
                if width < LANES:
                    near = jnp.where(lane < width, near, 0.0)
                results.append(bases[j] - ((6.0 + parts[j]) * d - near))
            for j, x in enumerate(xs):
                resid[x] = results[j]
            return carry

        by_chunks(level, body, 0, rows=512)

    def outside(level, r):
        first, second, width = blocks[level]
        faces_y, halo_x, halo_z, halo_y = level_refs[level][2:6]
        resid = level_refs[level][6]
        lane = lanes_of((second, LANES))
        resid[0] += jnp.where(has_lo["gx"], halo_x[r, 0], 0.0)
        resid[first - 1] += jnp.where(has_hi["gx"], halo_x[r, 1], 0.0)
        low = jnp.where(has_lo["gy"], halo_y[r, 0], 0.0)
        high = jnp.where(has_hi["gy"], halo_y[r, 1], 0.0)
        if width == LANES:
            low -= faces_y[r]
            high -= faces_y[r]
        ends = jnp.where(lane % 2 == 1, pltpu.roll(low, 1, 1), pltpu.roll(high, LANES - 1, 1))

        def add(x):
            res = resid[x]
            z_low = jnp.where(has_lo["gz"], halo_z[r, 0, pl.ds(x, 1), :], 0.0)
            z_high = jnp.where(has_hi["gz"], halo_z[r, 1, pl.ds(x, 1), :], 0.0)
            res = jnp.concatenate(
                (
                    res[:8] + jnp.where(edge_row == 0, z_low, 0.0),
                    res[8 : second - 8],
                    res[second - 8 :] + jnp.where(edge_row == 7, z_high, 0.0),
                )[:: 1 if second > 16 else 2],
                0,
            )
            to_low = pltpu.roll(ends, LANES - 1 - 2 * x, 1)
            if width == LANES:
                res += jnp.where((lane == 0) | (lane == LANES - 1), to_low, 0.0)
            else:
                to_high = pltpu.roll(ends, width - 1 - 2 * x, 1)
                res += jnp.where(lane == 0, to_low, jnp.where(lane == width - 1, to_high, 0.0))
            return res

        return add

    def smooth(level, source, coef, between):
        first, second, width = blocks[level]
        dirs, _, faces_y = level_refs[level][:3]
        resid, iterate = level_refs[level][6:8]
        upper = smooth_top + 4.0**level * absorb_top
        scale, firsts, seconds = cheb_tables(DEGREE + 1, smooth_low, upper)
        empty = jnp.zeros((second, LANES), jnp.float32)
        for r in range(DEGREE + 1):
            dirs[r, 0] = empty
            dirs[r, first + 1] = empty

        def opening(xs, packed):
            fields = [source[x] * scale for x in xs]
            for x, d in zip(xs, fields):
                iterate[x] = d
                packed = put_faces(level, 0, x, d, packed)
            return packed

        faces_y[0] = by_chunks(level, opening, empty)
        if level == 0:
            pl.semaphore_wait(barrier, len(z_peers) + len(plane_peers))
        start(level, 0, along_x)
        for r in range(DEGREE + 1):
            start(level, r, along_zy)
            if level == 0 and r == 0:
                fetches[1].wait()
            inside(level, r, source if r in (0, DEGREE) else resid, coef)
            if r in between:
                between[r]()
            arrive(level, r)
            add = outside(level, r)

            def last(xs, carry, add=add):
                results = [add(x) for x in xs]
                for x, res in zip(xs, results):
                    resid[x] = res
                return carry

            def turn(xs, packed, r=r, add=add):
                results = [add(x) for x in xs]
                fields = [
                    firsts[r] * dirs[r, x + 1] + seconds[r] * res for x, res in zip(xs, results)
                ]
                totals = [iterate[x] + d for x, d in zip(xs, fields)]
                for x, res, d, total in zip(xs, results, fields, totals):
                    resid[x] = res
                    iterate[x] = total
                    packed = put_faces(
                        level, r + 1, x, total if r == DEGREE - 1 else d, packed
                    )
                return packed

            if r == DEGREE:
                by_chunks(level, last, 0)
            else:
                faces_y[r + 1] = by_chunks(
                    level, turn, empty, lambda r=r: start(level, r + 1, along_x)
                )

    coef1, source1 = level_refs[1][8].at[0], level_refs[1][8].at[1]
    first2, second2, width2 = blocks[2]
    whole2 = (first2 * nx, second2 * nz, width2 * ny)
    whole3 = tuple(s // 2 for s in whole2)

    def spread(rows, shape, ref):
        for x in range(shape[0]):
            ref[x] = rows[x * shape[1] : (x + 1) * shape[1]]

    def into_message(rows):
        packed = rows[:second2]
        for x in range(1, first2):
            packed += pltpu.roll(rows[x * second2 : (x + 1) * second2], x * width2, 1)
        return packed

    def line(which, gath):
        piece = gath.at[me["gx"], me["gy"], me["gz"]]
        return gather(piece, which, z_peers, 0)

    def plane(which, gath):
        piece = gath.at[me["gx"], me["gy"]]
        return gather(piece, which, plane_peers, len(z_peers))

    def gather(piece, which, peers, base):
        return [
            pltpu.make_async_remote_copy(
                src_ref=piece,
                dst_ref=piece,
                send_sem=gsend.at[which, base + k],
                recv_sem=grecv.at[which, base + k],
                device_id=device(peer),
                device_id_type=MESH,
            )
            for k, peer in enumerate(peers)
        ]

    def begin(copies):
        for copy in copies:
            copy.start()

    def finish(copies):
        for copy in copies:
            copy.wait_recv()
        for copy in copies:
            copy.wait_send()

    def place(gath, ref):
        lane = lanes_of((second2, LANES))

        @pl.loop(0, nx * nz // 4)
        def _(n):
            for m in [4 * n + k for k in range(4)]:
                ix = m // nz
                iz = m % nz
                held = [gath[ix, iy, iz] for iy in range(ny)]
                for x in range(first2):
                    tile = jnp.zeros((second2, LANES), jnp.float32)
                    for iy in range(ny):
                        shift = (iy - x) * width2 % LANES
                        moved = pltpu.roll(held[iy], shift, 1) if shift else held[iy]
                        tile = jnp.where(lane // width2 == iy, moved, tile)
                    start_row = pl.multiple_of(iz * second2, second2)
                    ref[ix * first2 + x, pl.ds(start_row, second2), :] = tile

    def coarsen():
        spread(restrict(lambda x: ab[x], blocks[0]), blocks[1], coef1)
        rows = restrict(lambda x: coef1[x], blocks[1])
        gath_c[me["gx"], me["gy"], me["gz"]] = into_message(rows)
        begin(line(0, gath_c))

    def coarse_plane():
        finish(line(0, gath_c))
        begin(plane(0, gath_c))

    def coarse_all():
        finish(plane(0, gath_c))
        place(gath_c, coef2)

    def coarse_bottom():
        spread(restrict(lambda x: coef2[x], whole2), whole3, coef3)

    fetches[0].wait()
    smooth(0, rs, ab, {0: coarsen})
    keep0 = pltpu.make_async_copy(level_refs[0][7], out0, fetch_sem.at[2])
    keep0.start()
    resid = level_refs[0][6]
    spread(restrict(lambda x: resid[x], blocks[0]), blocks[1], source1)
    smooth(1, source1, coef1, {0: coarse_plane, 3: coarse_all, 4: coarse_bottom})
    rows = restrict(lambda x: level_refs[1][6][x], blocks[1])

    gath_s[me["gx"], me["gy"], me["gz"]] = into_message(rows)
    begin(line(1, gath_s))
    width1 = blocks[1][2]
    for x in range(blocks[1][0]):
        narrow[x] = level_refs[1][7][x][:, :width1]
    keep1 = pltpu.make_async_copy(narrow, out1, fetch_sem.at[3])
    keep1.start()
    finish(line(1, gath_s))
    begin(plane(1, gath_s))
    all_sent()
    finish(plane(1, gath_s))
    place(gath_s, src2)

    def neighbour_sum(below, d, above, width):
        second = d.shape[0]
        lane = lanes_of(d.shape)
        near = below + above
        up = pltpu.roll(d, 1, 0)
        down = pltpu.roll(d, second - 1, 0)
        up = jnp.concatenate((jnp.where(edge_row == 0, 0.0, up[:8]), up[8:]), 0)
        down = jnp.concatenate(
            (down[: second - 8], jnp.where(edge_row == 7, 0.0, down[second - 8 :])), 0
        )
        near += up + down
        left = pltpu.roll(d, 1, 1)
        right = pltpu.roll(d, LANES - 1, 1)
        if width == LANES:
            near += jnp.where(lane == 0, 0.0, left) + jnp.where(lane == LANES - 1, 0.0, right)
            return near
        return jnp.where(lane < width, near + left + right, 0.0)

    total_x, total_z, total_y = whole2
    zero = jnp.zeros((total_z, LANES), jnp.float32)
    scale, firsts, seconds = cheb_tables(
        DEGREE + 1, smooth_low, smooth_top + 4.0 ** (LEVELS - 1) * absorb_top
    )
    for slot in range(2):
        dir2[slot, 0] = zero
        dir2[slot, total_x + 1] = zero
    chunk = max(1, min(total_x, 256 // total_z))

    @pl.loop(0, total_x // chunk)
    def _(n):
        fields = [src2[n * chunk + j] * scale for j in range(chunk)]
        for j in range(chunk):
            dir2[0, n * chunk + j + 1] = fields[j]
            it2[n * chunk + j] = fields[j]

    for r in range(DEGREE + 1):
        old, new = r % 2, (r + 1) % 2

        @pl.loop(0, total_x // chunk)
        def _(n, r=r, old=old, new=new):
            xs = [n * chunk + j for j in range(chunk)]
            layers = [dir2[old, xs[0] + j] for j in range(chunk + 2)]
            bases = [(src2 if r in (0, DEGREE) else res2)[x] for x in xs]
            parts = [coef2[x] for x in xs]
            results = []
            for j in range(chunk):
                near = neighbour_sum(layers[j], layers[j + 1], layers[j + 2], total_y)
                results.append(bases[j] - ((6.0 + parts[j]) * layers[j + 1] - near))
            if r < DEGREE:
                fields = [
                    firsts[r] * layers[j + 1] + seconds[r] * results[j] for j in range(chunk)
                ]
                totals = [it2[x] + d for x, d in zip(xs, fields)]
                for j, x in enumerate(xs):
                    it2[x] = totals[j]
                    dir2[new, x + 1] = totals[j] if r == DEGREE - 1 else fields[j]
            for j, x in enumerate(xs):
                res2[x] = results[j]

    spread(restrict(lambda x: res2[x], whole2), whole3, src3)

    whole_x, whole_z, whole_y = whole3
    zero = jnp.zeros((whole_z, LANES), jnp.float32)
    for ref in (dir3, it3):
        ref[0] = zero
        ref[whole_x + 1] = zero
    for x in range(whole_x):
        source = src3[x]
        res3[x] = source
        dir3[x + 1] = source * bottom_scale
        it3[x + 1] = source * bottom_scale

    def bottom_turn(n, carry):
        one = tab[0, n]
        two = tab[1, n]
        layers = [dir3[x] for x in range(whole_x + 2)]
        bases = [res3[x] for x in range(whole_x)]
        for x in range(whole_x):
            near = neighbour_sum(layers[x], layers[x + 1], layers[x + 2], whole_y)
            res = bases[x] - ((6.0 + coef3[x]) * layers[x + 1] - near)
            d = one * layers[x + 1] + two * res
            res3[x] = res
            dir3[x + 1] = d
            it3[x + 1] += d
        return carry

    lax.fori_loop(0, BOTTOM_ITERS - 1, bottom_turn, 0)

    i = lanes_of((LANES, LANES))
    along_y = jnp.where(
        i < width2, trilinear(rows_of((LANES, LANES)), me["gy"] * width2 + i), 0.0
    )
    along_z = trilinear(
        lanes_of((second2, whole_z)), me["gz"] * second2 + rows_of((second2, whole_z))
    )
    layers = []
    for x in range(first2):
        centre = me["gx"] * (first2 // 2) + x // 2 + 1
        layers.append(0.75 * it3[centre] + 0.25 * it3[centre + 2 * (x % 2) - 1])
    moved = exact_dot(jnp.concatenate(layers, axis=0), along_y)
    own_rows = pl.ds(pl.multiple_of(me["gz"] * second2, second2), second2)
    back = lax.rem(LANES - me["gy"] * width2, LANES)
    for x in range(first2):
        fine = exact_dot(along_z, moved[x * whole_z : (x + 1) * whole_z])
        own = pltpu.roll(it2[me["gx"] * first2 + x, own_rows, :], back, 1)
        out2[x] = (own + fine)[:, :width2]
    keep0.wait()
    keep1.wait()


def on_device(sizes, right_side, absorption):
    nx, nz, ny = sizes
    blocks = [tuple(s // 2**k for s in right_side.shape) for k in range(LEVELS)]
    rounds = DEGREE + 1
    scratch = []
    for first, second, width in blocks[:SPLIT]:
        scratch += [
            pltpu.VMEM((rounds, first + 2, second, LANES), jnp.float32),
            pltpu.VMEM((rounds, 2, first, LANES), jnp.float32),
            pltpu.VMEM((rounds, second, LANES), jnp.float32),
            pltpu.VMEM((rounds, 2, second, LANES), jnp.float32),
            pltpu.VMEM((rounds, 2, first, LANES), jnp.float32),
            pltpu.VMEM((rounds, 2, second, LANES), jnp.float32),
            pltpu.VMEM((first, second, LANES), jnp.float32),
            pltpu.VMEM((first, second, LANES), jnp.float32),
            pltpu.VMEM((2, first, second, LANES), jnp.float32),
        ]
    first2, second2, _ = blocks[2]
    x2, z2 = first2 * nx, second2 * nz
    x3, z3 = x2 // 2, z2 // 2
    pair_rows = max(blocks[0][0] // 2 * blocks[0][1], x2 // 2 * z2)
    lines = nz - 1 + nx * ny - 1
    scratch += [
        pltpu.VMEM(right_side.shape, jnp.float32),
        pltpu.VMEM(right_side.shape, jnp.float32),
        pltpu.VMEM((pair_rows, LANES), jnp.float32),
        pltpu.VMEM((nx, ny, nz, second2, LANES), jnp.float32),
        pltpu.VMEM((nx, ny, nz, second2, LANES), jnp.float32),
        pltpu.VMEM((x2, z2, LANES), jnp.float32),
        pltpu.VMEM((x2, z2, LANES), jnp.float32),
        pltpu.VMEM((2, x2 + 2, z2, LANES), jnp.float32),
        pltpu.VMEM((x2, z2, LANES), jnp.float32),
        pltpu.VMEM((x2, z2, LANES), jnp.float32),
        pltpu.VMEM((x3, z3, LANES), jnp.float32),
        pltpu.VMEM((x3, z3, LANES), jnp.float32),
        pltpu.VMEM((x3 + 2, z3, LANES), jnp.float32),
        pltpu.VMEM((x3, z3, LANES), jnp.float32),
        pltpu.VMEM((x3 + 2, z3, LANES), jnp.float32),
        pltpu.SMEM((2, BOTTOM_ITERS - 1), jnp.float32),
        pltpu.SemaphoreType.DMA((SPLIT * rounds, 6)),
        pltpu.SemaphoreType.DMA((SPLIT * rounds, 6)),
        pltpu.SemaphoreType.DMA((2, lines)),
        pltpu.SemaphoreType.DMA((2, lines)),
        pltpu.SemaphoreType.DMA((4,)),
        pltpu.VMEM(blocks[1], jnp.float32),
    ]
    vmem = pl.BlockSpec(memory_space=pltpu.VMEM)
    hbm = pl.BlockSpec(memory_space=pltpu.HBM)
    return pl.pallas_call(
        functools.partial(kernel, sizes, blocks),
        out_shape=tuple(jax.ShapeDtypeStruct(b, jnp.float32) for b in blocks),
        in_specs=[hbm, hbm],
        out_specs=(hbm, hbm, vmem),
        scratch_shapes=scratch,
        compiler_params=pltpu.CompilerParams(
            collective_id=0, has_side_effects=True, vmem_limit_bytes=63 * 1024 * 1024
        ),
    )(right_side, absorption)


def solution(mesh):
    sizes = tuple(mesh.shape[a] for a in AXES)
    spec = P("gx", "gz", "gy")
    return jax.shard_map(
        functools.partial(on_device, sizes),
        mesh=mesh,
        in_specs=(spec, spec),
        out_specs=(spec, spec, spec),
        check_vma=False,
    )
```

```python
import functools

import jax
import jax.numpy as jnp
from jax import lax
from jax.experimental import pallas as pl
from jax.experimental.pallas import tpu as pltpu
from jax.sharding import PartitionSpec as P

DEGREE = 4
LEVELS = 3
SPLIT = 2
BOTTOM_ITERS = 20
LANES = 128

smooth_low = 1.5
smooth_top = 12.0
absorb_top = 1.0
bottom_low = 0.008

MESH = pl.DeviceIdType.MESH
AXES = ("gx", "gz", "gy")


def cheb_tables(count, lower, upper):
    theta = (upper + lower) / 2.0
    delta = (upper - lower) / 2.0
    sigma = theta / delta
    rho_value = 1.0 / sigma
    firsts = []
    seconds = []
    for turn_index in range(count - 1):
        rho_next = 1.0 / (2.0 * sigma - rho_value)
        firsts.append(rho_next * rho_value)
        seconds.append(2.0 * rho_next / delta)
        rho_value = rho_next
    return (1.0 / theta, firsts, seconds)


def exact_dot(left, right):
    return jnp.dot(
        left, right, precision=lax.Precision.HIGHEST, preferred_element_type=jnp.float32
    )


def lanes_of(shape):
    return lax.broadcasted_iota(jnp.int32, shape, len(shape) - 1)


def rows_of(shape):
    return lax.broadcasted_iota(jnp.int32, shape, len(shape) - 2)


def halving():
    j = rows_of((LANES, LANES))
    i = lanes_of((LANES, LANES))
    return jnp.where(j // 2 == i, jnp.float32(0.5), jnp.float32(0.0))


def trilinear(coarse, fine):
    centre = fine // 2
    other = centre + 2 * (fine % 2) - 1
    return jnp.where(coarse == centre, jnp.float32(0.75), jnp.float32(0.0)) + jnp.where(
        coarse == other, jnp.float32(0.25), jnp.float32(0.0)
    )


def kernel(sizes, blocks, rs_hbm, ab_hbm, out0, out1, out2, *scratch):
    nx, nz, ny = sizes
    me = {a: lax.axis_index(a) for a in AXES}
    count = dict(zip(AXES, sizes))
    has_lo = {a: me[a] > 0 for a in AXES}
    has_hi = {a: me[a] < count[a] - 1 for a in AXES}

    per_level = 9
    level_refs = [list(scratch[per_level * k : per_level * (k + 1)]) for k in range(SPLIT)]
    rest = scratch[per_level * SPLIT :]
    rs, ab, pairs, gath_s, gath_c, src2, coef2, dir2, res2, it2 = rest[:10]
    src3, coef3, dir3, res3, it3, tab = rest[10:16]
    send_sem, recv_sem, gsend, grecv, fetch_sem, narrow = rest[16:]

    fetches = [
        pltpu.make_async_copy(rs_hbm, rs, fetch_sem.at[0]),
        pltpu.make_async_copy(ab_hbm, ab, fetch_sem.at[1]),
    ]
    for fetch in fetches:
        fetch.start()

    bottom_scale, firsts, seconds = cheb_tables(
        BOTTOM_ITERS, bottom_low, smooth_top + 4.0**LEVELS * absorb_top
    )
    for n in range(BOTTOM_ITERS - 1):
        tab[0, n] = jnp.float32(firsts[n])
        tab[1, n] = jnp.float32(seconds[n])

    z_peers = [{"gz": k} for k in range(1, nz)]
    plane_peers = [
        {"gx": i, "gy": j} for i in range(nx) for j in range(ny) if (i, j) != (0, 0)
    ]

    def device(offsets):
        return {a: lax.rem(me[a] + k, count[a]) for a, k in offsets.items()}

    barrier = pltpu.get_barrier_semaphore()
    for peer in z_peers + plane_peers:
        pl.semaphore_signal(barrier, inc=1, device_id=device(peer), device_id_type=MESH)

    half = halving()

    def restrict(read, shape):
        first, second, _ = shape
        for x in range(first // 2):
            pairs[pl.ds(x * second, second), :] = read(2 * x) + read(2 * x + 1)
        total = first // 2 * second // 2
        summed = (
            pairs[pl.ds(0, total, stride=2), :] + pairs[pl.ds(1, total, stride=2), :]
        )
        return exact_dot(summed, half)

    def copies(level, r):
        first, second, _ = blocks[level]
        dirs, faces_z, faces_y, halo_x, halo_z, halo_y = level_refs[level][:6]
        slot = level * (DEGREE + 1) + r
        ends = {
            "gx": (dirs.at[r, 1], dirs.at[r, first], halo_x),
            "gz": (faces_z.at[r, 0], faces_z.at[r, 1], halo_z),
            "gy": (faces_y.at[r], faces_y.at[r], halo_y),
        }
        made = []
        for n, a in enumerate(AXES):
            low_face, high_face, halo = ends[a]
            made.append(
                (
                    has_lo[a],
                    has_hi[a],
                    pltpu.make_async_remote_copy(
                        src_ref=low_face,
                        dst_ref=halo.at[r, 1],
                        send_sem=send_sem.at[slot, 2 * n],
                        recv_sem=recv_sem.at[slot, 2 * n],
                        device_id={a: jnp.maximum(me[a] - 1, 0)},
                        device_id_type=MESH,
                    ),
                )
            )
            made.append(
                (
                    has_hi[a],
                    has_lo[a],
                    pltpu.make_async_remote_copy(
                        src_ref=high_face,
                        dst_ref=halo.at[r, 0],
                        send_sem=send_sem.at[slot, 2 * n + 1],
                        recv_sem=recv_sem.at[slot, 2 * n + 1],
                        device_id={a: jnp.minimum(me[a] + 1, count[a] - 1)},
                        device_id_type=MESH,
                    ),
                )
            )
        return made

    def start(level, r, part):
        for sends, _, copy in copies(level, r)[part]:
            pl.when(sends)(copy.start)

    along_x, along_zy = slice(0, 2), slice(2, 6)

    def arrive(level, r):
        for _, gets, copy in copies(level, r):
            pl.when(gets)(copy.wait_recv)

    def all_sent():
        rounds = [copies(level, r) for level in range(SPLIT) for r in range(DEGREE + 1)]
        for way in range(6):

            @pl.when(rounds[0][way][0])
            def _(way=way):
                for made in rounds:
                    made[way][2].wait_send()

    def put_faces(level, r, x, field, packed):
        second, width = blocks[level][1:]
        dirs, faces_z = level_refs[level][:2]
        dirs[r, x + 1] = field
        faces_z[r, 0, pl.ds(x, 1), :] = field[:1]
        faces_z[r, 1, pl.ds(x, 1), :] = field[second - 1 :]
        lane = lanes_of((second, LANES))
        low = pltpu.roll(field, 2 * x + 1, 1)
        if width == LANES:
            return jnp.where(lane // 2 == x, low, packed)
        high = pltpu.roll(field, 2 * x + LANES + 1 - width, 1)
        return jnp.where(lane == 2 * x + 1, low, jnp.where(lane == 2 * x, high, packed))

    def by_chunks(level, body, carry, ends_done=None, rows=256):
        first, second, _ = blocks[level]
        chunk = min(first, rows // second)
        turns = first // chunk

        def turn(n, carry):
            if turns > 2:
                chosen = jnp.where(n == 0, 0, jnp.where(n == 1, turns - 1, n - 1))
            else:
                chosen = n
            carry = body([chosen * chunk + j for j in range(chunk)], carry)
            if ends_done is not None and turns > 1:
                pl.when(n == 1)(ends_done)
            return carry

        if turns == 1:
            carry = turn(0, carry)
            if ends_done is not None:
                ends_done()
            return carry
        return lax.fori_loop(0, turns, turn, carry)

    edge_row = rows_of((8, LANES))

    def inside(level, r, base, coef):
        first, second, width = blocks[level]
        dirs = level_refs[level][0]
        resid = level_refs[level][6]
        lane = lanes_of((second, LANES))

        def body(xs, carry):
            layers = [dirs[r, xs[0] + j] for j in range(len(xs) + 2)]
            bases = [base[x] for x in xs]
            parts = [coef[x] for x in xs]
            results = []
            for j in range(len(xs)):
                d = layers[j + 1]
                near = layers[j] + layers[j + 2]
                up = pltpu.roll(d, 1, 0)
                down = pltpu.roll(d, second - 1, 0)
                up = jnp.concatenate((jnp.where(edge_row == 0, 0.0, up[:8]), up[8:]), 0)
                down = jnp.concatenate(
                    (down[: second - 8], jnp.where(edge_row == 7, 0.0, down[second - 8 :])), 0
                )
                near += up + down
                near += pltpu.roll(d, 1, 1) + pltpu.roll(d, LANES - 1, 1)
                if width < LANES:
                    near = jnp.where(lane < width, near, 0.0)
                results.append(bases[j] - ((6.0 + parts[j]) * d - near))
            for j, x in enumerate(xs):
                resid[x] = results[j]
            return carry

        by_chunks(level, body, 0)

    def outside(level, r):
        first, second, width = blocks[level]
        faces_y, halo_x, halo_z, halo_y = level_refs[level][2:6]
        resid = level_refs[level][6]
        lane = lanes_of((second, LANES))
        resid[0] += jnp.where(has_lo["gx"], halo_x[r, 0], 0.0)
        resid[first - 1] += jnp.where(has_hi["gx"], halo_x[r, 1], 0.0)
        low = jnp.where(has_lo["gy"], halo_y[r, 0], 0.0)
        high = jnp.where(has_hi["gy"], halo_y[r, 1], 0.0)
        if width == LANES:
            low -= faces_y[r]
            high -= faces_y[r]
        ends = jnp.where(lane % 2 == 1, pltpu.roll(low, 1, 1), pltpu.roll(high, LANES - 1, 1))

        def add(x):
            res = resid[x]
            z_low = jnp.where(has_lo["gz"], halo_z[r, 0, pl.ds(x, 1), :], 0.0)
            z_high = jnp.where(has_hi["gz"], halo_z[r, 1, pl.ds(x, 1), :], 0.0)
            res = jnp.concatenate(
                (
                    res[:8] + jnp.where(edge_row == 0, z_low, 0.0),
                    res[8 : second - 8],
                    res[second - 8 :] + jnp.where(edge_row == 7, z_high, 0.0),
                )[:: 1 if second > 16 else 2],
                0,
            )
            to_low = pltpu.roll(ends, LANES - 1 - 2 * x, 1)
            if width == LANES:
                res += jnp.where((lane == 0) | (lane == LANES - 1), to_low, 0.0)
            else:
                to_high = pltpu.roll(ends, width - 1 - 2 * x, 1)
                res += jnp.where(lane == 0, to_low, jnp.where(lane == width - 1, to_high, 0.0))
            return res

        return add

    def smooth(level, source, coef, between):
        first, second, width = blocks[level]
        dirs, _, faces_y = level_refs[level][:3]
        resid, iterate = level_refs[level][6:8]
        upper = smooth_top + 4.0**level * absorb_top
        scale, firsts, seconds = cheb_tables(DEGREE + 1, smooth_low, upper)
        empty = jnp.zeros((second, LANES), jnp.float32)
        for r in range(DEGREE + 1):
            dirs[r, 0] = empty
            dirs[r, first + 1] = empty

        def opening(xs, packed):
            fields = [source[x] * scale for x in xs]
            for x, d in zip(xs, fields):
                iterate[x] = d
                packed = put_faces(level, 0, x, d, packed)
            return packed

        faces_y[0] = by_chunks(level, opening, empty)
        if level == 0:
            pl.semaphore_wait(barrier, len(z_peers) + len(plane_peers))
        start(level, 0, along_x)
        for r in range(DEGREE + 1):
            start(level, r, along_zy)
            if level == 0 and r == 0:
                fetches[1].wait()
            inside(level, r, source if r in (0, DEGREE) else resid, coef)
            if r in between:
                between[r]()
            arrive(level, r)
            add = outside(level, r)

            def last(xs, carry, add=add):
                results = [add(x) for x in xs]
                for x, res in zip(xs, results):
                    resid[x] = res
                return carry

            def turn(xs, packed, r=r, add=add):
                results = [add(x) for x in xs]
                fields = [
                    firsts[r] * dirs[r, x + 1] + seconds[r] * res for x, res in zip(xs, results)
                ]
                totals = [iterate[x] + d for x, d in zip(xs, fields)]
                for x, res, d, total in zip(xs, results, fields, totals):
                    resid[x] = res
                    iterate[x] = total
                    packed = put_faces(
                        level, r + 1, x, total if r == DEGREE - 1 else d, packed
                    )
                return packed

            if r == DEGREE:
                by_chunks(level, last, 0)
            else:
                faces_y[r + 1] = by_chunks(
                    level, turn, empty, lambda r=r: start(level, r + 1, along_x)
                )

    coef1, source1 = level_refs[1][8].at[0], level_refs[1][8].at[1]
    first2, second2, width2 = blocks[2]
    whole2 = (first2 * nx, second2 * nz, width2 * ny)
    whole3 = tuple(s // 2 for s in whole2)

    def spread(rows, shape, ref):
        for x in range(shape[0]):
            ref[x] = rows[x * shape[1] : (x + 1) * shape[1]]

    def into_message(rows):
        packed = rows[:second2]
        for x in range(1, first2):
            packed += pltpu.roll(rows[x * second2 : (x + 1) * second2], x * width2, 1)
        return packed

    def line(which, gath):
        piece = gath.at[me["gx"], me["gy"], me["gz"]]
        return gather(piece, which, z_peers, 0)

    def plane(which, gath):
        piece = gath.at[me["gx"], me["gy"]]
        return gather(piece, which, plane_peers, len(z_peers))

    def gather(piece, which, peers, base):
        return [
            pltpu.make_async_remote_copy(
                src_ref=piece,
                dst_ref=piece,
                send_sem=gsend.at[which, base + k],
                recv_sem=grecv.at[which, base + k],
                device_id=device(peer),
                device_id_type=MESH,
            )
            for k, peer in enumerate(peers)
        ]

    def begin(copies):
        for copy in copies:
            copy.start()

    def finish(copies):
        for copy in copies:
            copy.wait_recv()
        for copy in copies:
            copy.wait_send()

    def place(gath, ref):
        lane = lanes_of((second2, LANES))

        @pl.loop(0, nx * nz // 4)
        def _(n):
            for m in [4 * n + k for k in range(4)]:
                ix = m // nz
                iz = m % nz
                held = [gath[ix, iy, iz] for iy in range(ny)]
                for x in range(first2):
                    tile = jnp.zeros((second2, LANES), jnp.float32)
                    for iy in range(ny):
                        shift = (iy - x) * width2 % LANES
                        moved = pltpu.roll(held[iy], shift, 1) if shift else held[iy]
                        tile = jnp.where(lane // width2 == iy, moved, tile)
                    start_row = pl.multiple_of(iz * second2, second2)
                    ref[ix * first2 + x, pl.ds(start_row, second2), :] = tile

    def coarsen():
        spread(restrict(lambda x: ab[x], blocks[0]), blocks[1], coef1)

    def coarsen_again():
        rows = restrict(lambda x: coef1[x], blocks[1])
        gath_c[me["gx"], me["gy"], me["gz"]] = into_message(rows)
        begin(line(0, gath_c))

    def coarse_plane():
        finish(line(0, gath_c))
        begin(plane(0, gath_c))

    def coarse_all():
        finish(plane(0, gath_c))
        place(gath_c, coef2)

    def coarse_bottom():
        spread(restrict(lambda x: coef2[x], whole2), whole3, coef3)

    fetches[0].wait()
    smooth(0, rs, ab, {0: coarsen, 1: coarsen_again})
    keep0 = pltpu.make_async_copy(level_refs[0][7], out0, fetch_sem.at[2])
    keep0.start()
    resid = level_refs[0][6]
    spread(restrict(lambda x: resid[x], blocks[0]), blocks[1], source1)
    smooth(1, source1, coef1, {0: coarse_plane, 3: coarse_all, 4: coarse_bottom})
    rows = restrict(lambda x: level_refs[1][6][x], blocks[1])

    gath_s[me["gx"], me["gy"], me["gz"]] = into_message(rows)
    begin(line(1, gath_s))
    width1 = blocks[1][2]
    for x in range(blocks[1][0]):
        narrow[x] = level_refs[1][7][x][:, :width1]
    keep1 = pltpu.make_async_copy(narrow, out1, fetch_sem.at[3])
    keep1.start()
    finish(line(1, gath_s))
    begin(plane(1, gath_s))
    all_sent()
    finish(plane(1, gath_s))
    place(gath_s, src2)

    def neighbour_sum(below, d, above, width):
        second = d.shape[0]
        lane = lanes_of(d.shape)
        near = below + above
        up = pltpu.roll(d, 1, 0)
        down = pltpu.roll(d, second - 1, 0)
        up = jnp.concatenate((jnp.where(edge_row == 0, 0.0, up[:8]), up[8:]), 0)
        down = jnp.concatenate(
            (down[: second - 8], jnp.where(edge_row == 7, 0.0, down[second - 8 :])), 0
        )
        near += up + down
        left = pltpu.roll(d, 1, 1)
        right = pltpu.roll(d, LANES - 1, 1)
        if width == LANES:
            near += jnp.where(lane == 0, 0.0, left) + jnp.where(lane == LANES - 1, 0.0, right)
            return near
        return jnp.where(lane < width, near + left + right, 0.0)

    total_x, total_z, total_y = whole2
    zero = jnp.zeros((total_z, LANES), jnp.float32)
    scale, firsts, seconds = cheb_tables(
        DEGREE + 1, smooth_low, smooth_top + 4.0 ** (LEVELS - 1) * absorb_top
    )
    for slot in range(2):
        dir2[slot, 0] = zero
        dir2[slot, total_x + 1] = zero
    chunk = max(1, min(total_x, 256 // total_z))

    @pl.loop(0, total_x // chunk)
    def _(n):
        fields = [src2[n * chunk + j] * scale for j in range(chunk)]
        for j in range(chunk):
            dir2[0, n * chunk + j + 1] = fields[j]
            it2[n * chunk + j] = fields[j]

    for r in range(DEGREE + 1):
        old, new = r % 2, (r + 1) % 2

        @pl.loop(0, total_x // chunk)
        def _(n, r=r, old=old, new=new):
            xs = [n * chunk + j for j in range(chunk)]
            layers = [dir2[old, xs[0] + j] for j in range(chunk + 2)]
            bases = [(src2 if r in (0, DEGREE) else res2)[x] for x in xs]
            parts = [coef2[x] for x in xs]
            results = []
            for j in range(chunk):
                near = neighbour_sum(layers[j], layers[j + 1], layers[j + 2], total_y)
                results.append(bases[j] - ((6.0 + parts[j]) * layers[j + 1] - near))
            if r < DEGREE:
                fields = [
                    firsts[r] * layers[j + 1] + seconds[r] * results[j] for j in range(chunk)
                ]
                totals = [it2[x] + d for x, d in zip(xs, fields)]
                for j, x in enumerate(xs):
                    it2[x] = totals[j]
                    dir2[new, x + 1] = totals[j] if r == DEGREE - 1 else fields[j]
            for j, x in enumerate(xs):
                res2[x] = results[j]

    spread(restrict(lambda x: res2[x], whole2), whole3, src3)

    whole_x, whole_z, whole_y = whole3
    zero = jnp.zeros((whole_z, LANES), jnp.float32)
    for ref in (dir3, it3):
        ref[0] = zero
        ref[whole_x + 1] = zero
    for x in range(whole_x):
        source = src3[x]
        res3[x] = source
        dir3[x + 1] = source * bottom_scale
        it3[x + 1] = source * bottom_scale

    def bottom_turn(n, carry):
        one = tab[0, n]
        two = tab[1, n]
        layers = [dir3[x] for x in range(whole_x + 2)]
        bases = [res3[x] for x in range(whole_x)]
        for x in range(whole_x):
            near = neighbour_sum(layers[x], layers[x + 1], layers[x + 2], whole_y)
            res = bases[x] - ((6.0 + coef3[x]) * layers[x + 1] - near)
            d = one * layers[x + 1] + two * res
            res3[x] = res
            dir3[x + 1] = d
            it3[x + 1] += d
        return carry

    lax.fori_loop(0, BOTTOM_ITERS - 1, bottom_turn, 0)

    i = lanes_of((LANES, LANES))
    along_y = jnp.where(
        i < width2, trilinear(rows_of((LANES, LANES)), me["gy"] * width2 + i), 0.0
    )
    along_z = trilinear(
        lanes_of((second2, whole_z)), me["gz"] * second2 + rows_of((second2, whole_z))
    )
    layers = []
    for x in range(first2):
        centre = me["gx"] * (first2 // 2) + x // 2 + 1
        layers.append(0.75 * it3[centre] + 0.25 * it3[centre + 2 * (x % 2) - 1])
    moved = exact_dot(jnp.concatenate(layers, axis=0), along_y)
    own_rows = pl.ds(pl.multiple_of(me["gz"] * second2, second2), second2)
    back = lax.rem(LANES - me["gy"] * width2, LANES)
    for x in range(first2):
        fine = exact_dot(along_z, moved[x * whole_z : (x + 1) * whole_z])
        own = pltpu.roll(it2[me["gx"] * first2 + x, own_rows, :], back, 1)
        out2[x] = (own + fine)[:, :width2]
    keep0.wait()
    keep1.wait()


def on_device(sizes, right_side, absorption):
    nx, nz, ny = sizes
    blocks = [tuple(s // 2**k for s in right_side.shape) for k in range(LEVELS)]
    rounds = DEGREE + 1
    scratch = []
    for first, second, width in blocks[:SPLIT]:
        scratch += [
            pltpu.VMEM((rounds, first + 2, second, LANES), jnp.float32),
            pltpu.VMEM((rounds, 2, first, LANES), jnp.float32),
            pltpu.VMEM((rounds, second, LANES), jnp.float32),
            pltpu.VMEM((rounds, 2, second, LANES), jnp.float32),
            pltpu.VMEM((rounds, 2, first, LANES), jnp.float32),
            pltpu.VMEM((rounds, 2, second, LANES), jnp.float32),
            pltpu.VMEM((first, second, LANES), jnp.float32),
            pltpu.VMEM((first, second, LANES), jnp.float32),
            pltpu.VMEM((2, first, second, LANES), jnp.float32),
        ]
    first2, second2, _ = blocks[2]
    x2, z2 = first2 * nx, second2 * nz
    x3, z3 = x2 // 2, z2 // 2
    pair_rows = max(blocks[0][0] // 2 * blocks[0][1], x2 // 2 * z2)
    lines = nz - 1 + nx * ny - 1
    scratch += [
        pltpu.VMEM(right_side.shape, jnp.float32),
        pltpu.VMEM(right_side.shape, jnp.float32),
        pltpu.VMEM((pair_rows, LANES), jnp.float32),
        pltpu.VMEM((nx, ny, nz, second2, LANES), jnp.float32),
        pltpu.VMEM((nx, ny, nz, second2, LANES), jnp.float32),
        pltpu.VMEM((x2, z2, LANES), jnp.float32),
        pltpu.VMEM((x2, z2, LANES), jnp.float32),
        pltpu.VMEM((2, x2 + 2, z2, LANES), jnp.float32),
        pltpu.VMEM((x2, z2, LANES), jnp.float32),
        pltpu.VMEM((x2, z2, LANES), jnp.float32),
        pltpu.VMEM((x3, z3, LANES), jnp.float32),
        pltpu.VMEM((x3, z3, LANES), jnp.float32),
        pltpu.VMEM((x3 + 2, z3, LANES), jnp.float32),
        pltpu.VMEM((x3, z3, LANES), jnp.float32),
        pltpu.VMEM((x3 + 2, z3, LANES), jnp.float32),
        pltpu.SMEM((2, BOTTOM_ITERS - 1), jnp.float32),
        pltpu.SemaphoreType.DMA((SPLIT * rounds, 6)),
        pltpu.SemaphoreType.DMA((SPLIT * rounds, 6)),
        pltpu.SemaphoreType.DMA((2, lines)),
        pltpu.SemaphoreType.DMA((2, lines)),
        pltpu.SemaphoreType.DMA((4,)),
        pltpu.VMEM(blocks[1], jnp.float32),
    ]
    vmem = pl.BlockSpec(memory_space=pltpu.VMEM)
    hbm = pl.BlockSpec(memory_space=pltpu.HBM)
    return pl.pallas_call(
        functools.partial(kernel, sizes, blocks),
        out_shape=tuple(jax.ShapeDtypeStruct(b, jnp.float32) for b in blocks),
        in_specs=[hbm, hbm],
        out_specs=(hbm, hbm, vmem),
        scratch_shapes=scratch,
        compiler_params=pltpu.CompilerParams(
            collective_id=0, has_side_effects=True, vmem_limit_bytes=63 * 1024 * 1024
        ),
    )(right_side, absorption)


def solution(mesh):
    sizes = tuple(mesh.shape[a] for a in AXES)
    spec = P("gx", "gz", "gy")
    return jax.shard_map(
        functools.partial(on_device, sizes),
        mesh=mesh,
        in_specs=(spec, spec),
        out_specs=(spec, spec, spec),
        check_vma=False,
    )
```
